512 devices in a mesh: freq: 128 (over z, y, core), pol: 4 (over x).
Axes of the slice: x: 4, y: 8, z: 8, core: 2. Of those that a mesh axis runs over, the one named last changes fastest.
Arguments:
- voltages: bfloat16 [128, 4, 1392, 2, 512], P('freq', 'pol'), as said below
- gains: float32 [128, 4, 2, 512], P('freq', 'pol'), as said below
- slopes: int32 [2048], replicated, may hold values from 0 to 48, as said below
- mask: int32 [2048], replicated, may hold values from 0 to 1, as said below
Outputs:
- dedispersed: float32 [1024, 24, 96], P('freq', None, 'pol')
The draws below stay inside these ranges and needn't reach their ends.
Inputs may be any that keep to these rules, and one draw needn't show every extreme that they name: `voltages`: real and imaginary parts of each feed's voltage in each coarse channel, group and sample. `gains`: complex gain of each feed in each coarse channel and group. `slopes`: some fine channel has the slope 48. `mask`: 1 marks a live fine channel; the middle fine channel is live.
All inputs are finite; a program needn't handle non-finite values.
Results may differ from the reference program's by a relative error of at most 0.025.
The reference program's roundings to bfloat16 on the way count: a program that leaves them out, or rounds other values in their place, can miss the bound.
Values may be sent and summed in bfloat16 or wider, within the bound.
No kernel may reach another device: no remote copies, remote signals or barrier semaphores. Data moves between devices by JAX's collectives and lax.ppermute only.
A program may use at most 64 MiB of HBM per device.

```python
import math
import jax
import jax.numpy as jnp
from jax import lax

FEED_G = 512
BEAMS = 1024
GROUPS = 4
UP = 16
TAPS = 16
DM = 96
MAXD = 48
TOUT = 24
CH_DEV = 1
FR = 72
TS = 1392
CH = 128


def gain_values(key, uniform_width, level_log):
    key_one, key_two, key_three, key_four = jax.random.split(jax.random.fold_in(key, 11), 4)
    shape = (CH, GROUPS, 2, FEED_G)
    base_draw = jax.random.normal(key_one, shape, jnp.float32)
    base_draw = base_draw + jax.random.uniform(key_four, shape, jnp.float32, -uniform_width, uniform_width)
    channel_level = jnp.exp(jax.random.uniform(key_two, (CH, 1, 1, 1), jnp.float32, 0.0, level_log))
    group_level = 1.0 + 2.0 * jnp.arange(GROUPS, dtype=jnp.float32) / (GROUPS - 1)
    feed_level = 0.5 + jax.random.uniform(key_three, (1, 1, 1, FEED_G), jnp.float32)
    return base_draw * jnp.sqrt(channel_level) * jnp.sqrt(group_level)[None, :, None, None] * feed_level


def draw_gains(key, part):
    return gain_values(key, 0.0, math.log(10.0))


def draw_voltages(key, part):
    shape = (CH, GROUPS, TS, 2, FEED_G)
    gain_draw = gain_values(key, 0.0, math.log(10.0))
    key = jax.random.fold_in(key, 5)
    key_noise, key_source, key_beam = jax.random.split(key, 3)
    noise = jax.random.normal(key_noise, shape, jnp.float32)
    strength = 0.1
    real_g = gain_draw[:, :, 0, :]
    imag_g = gain_draw[:, :, 1, :]
    magnitude = jnp.sqrt(real_g * real_g + imag_g * imag_g + 1e-12)
    unit_re = real_g / magnitude
    unit_im = -imag_g / magnitude
    owner_count = CH // CH_DEV
    owner_width = BEAMS // owner_count
    channel_owner = jnp.arange(CH, dtype=jnp.int32) // CH_DEV
    far_owner = (channel_owner + owner_count // 2) % owner_count
    beam_offset = jax.random.randint(key_beam, (CH,), 0, owner_width, dtype=jnp.int32)
    source_beam = (far_owner * owner_width + beam_offset).reshape(CH, 1, 1)
    feed_index = jnp.arange(FEED_G, dtype=jnp.int32)[None, None, :]
    angle = (feed_index * source_beam % BEAMS).astype(jnp.float32) * (2.0 * math.pi / BEAMS)
    ramp_re = jnp.cos(angle)
    ramp_im = jnp.sin(angle)
    steer_re = (ramp_re * unit_re - ramp_im * unit_im)[:, :, None, :]
    steer_im = (ramp_re * unit_im + ramp_im * unit_re)[:, :, None, :]
    source_time = strength * math.sqrt(0.5) * jax.random.normal(key_source, (CH, GROUPS, TS, 2), jnp.float32)
    source_re = source_time[..., 0:1]
    source_im = source_time[..., 1:2]
    wave_re = source_re * steer_re - source_im * steer_im
    wave_im = source_re * steer_im + source_im * steer_re
    source = jnp.stack([wave_re, wave_im], axis=3)
    return jnp.clip(noise + source, -6.0, 6.0).astype(jnp.bfloat16)


def draw_slopes(key, part):
    key_one, key_two = jax.random.split(jax.random.fold_in(key, 23), 2)
    cell_count = CH * UP
    drawn_slopes = jax.random.randint(key_one, (cell_count,), 0, MAXD + 1, dtype=jnp.int32)
    steep_channel = jax.random.randint(key_two, (), 0, cell_count, dtype=jnp.int32)
    cell_index = jnp.arange(cell_count, dtype=jnp.int32)
    return jnp.where(cell_index == steep_channel, MAXD, drawn_slopes).astype(jnp.int32)


def draw_mask(key, part):
    key_one, key_two, key_three = jax.random.split(jax.random.fold_in(key, 37), 3)
    cell_count = CH * UP
    low_edge = jax.random.randint(key_one, (), 0, cell_count // 8, dtype=jnp.int32)
    high_edge = jax.random.randint(key_two, (), 0, cell_count // 8, dtype=jnp.int32)
    rfi_draw = jax.random.randint(key_three, (cell_count,), 0, 6, dtype=jnp.int32)
    cell_index = jnp.arange(cell_count, dtype=jnp.int32)
    live_channels = (cell_index >= low_edge) & (cell_index < cell_count - high_edge) & (rfi_draw != 0)
    live_channels = live_channels | (cell_index == cell_count // 2)
    return live_channels.astype(jnp.int32)


def setup_inputs(seed: int = 0) -> dict:
    seeds = jax.random.split(jax.random.key(seed), 5)
    voltages = draw_voltages(jax.random.fold_in(seeds[4], 71), 0)
    gains = draw_gains(jax.random.fold_in(seeds[4], 71), 0)
    slopes = draw_slopes(jax.random.fold_in(seeds[4], 71), 0)
    mask = draw_mask(jax.random.fold_in(seeds[4], 71), 0)
    return dict(voltages=voltages, gains=gains, slopes=slopes, mask=mask)


EPSILON = 1e-06
HIGHEST = lax.Precision.HIGHEST

def beam_table(feed_count, beam_order):
    feed_index = jnp.arange(feed_count, dtype=jnp.int32)[:, None]
    turn_count = feed_index * beam_order[None, :] % BEAMS
    angles = turn_count.astype(jnp.float32) * (2.0 * math.pi / BEAMS)
    norm_scale = 1.0 / math.sqrt(feed_count)
    cosine = jnp.cos(angles) * norm_scale
    sine_table = jnp.sin(angles) * norm_scale
    top_rows = jnp.concatenate([cosine, -sine_table], axis=1)
    bottom_rows = jnp.concatenate([sine_table, cosine], axis=1)
    return jnp.concatenate([top_rows, bottom_rows], axis=0).astype(jnp.bfloat16)

def filter_taps():
    length = TAPS * UP
    position = jnp.arange(length, dtype=jnp.float32) + 0.5
    hann_window = 0.5 - 0.5 * jnp.cos(2.0 * math.pi * position / length)
    values = jnp.sinc((position - 0.5 * length) / UP) * hann_window
    return values.reshape(TAPS, UP).astype(jnp.bfloat16)

def band_matrix(block_count):
    coeffs = filter_taps().astype(jnp.float32)
    time_lag = jnp.arange(block_count, dtype=jnp.int32)[None, :] - jnp.arange(FR, dtype=jnp.int32)[:, None]
    select = (time_lag[None, :, :] == jnp.arange(TAPS, dtype=jnp.int32)[:, None, None]).astype(jnp.float32)
    return jnp.einsum('pn,pmq->nmq', coeffs, select, precision=HIGHEST).astype(jnp.bfloat16)

def fourier_tables():
    freq_index = jnp.arange(UP, dtype=jnp.int32)
    turn_count = freq_index[:, None] * freq_index[None, :] % UP
    angles = turn_count.astype(jnp.float32) * (2.0 * math.pi / UP)
    return (jnp.cos(angles), jnp.sin(angles))

def calibrate(voltage, gain_group):
    real_v = voltage[:, :, 0, :].astype(jnp.float32)
    imag_v = voltage[:, :, 1, :].astype(jnp.float32)
    real_g = gain_group[:, None, 0, :]
    imag_g = gain_group[:, None, 1, :]
    real_x = real_v * real_g - imag_v * imag_g
    imag_x = real_v * imag_g + imag_v * real_g
    return jnp.concatenate([real_x, imag_x], axis=-1).astype(jnp.bfloat16)

def fine_power(formed):
    group_count = formed.shape[0]
    block_count = formed.shape[1] // UP
    blocks = formed.reshape(group_count, block_count, UP, 2 * BEAMS).astype(jnp.float32)
    windowed = jnp.einsum('cqnb,nmq->cmnb', blocks, band_matrix(block_count).astype(jnp.float32), precision=HIGHEST)
    cosine, sine_table = fourier_tables()
    real_in = windowed[..., :BEAMS]
    imag_in = windowed[..., BEAMS:]
    real_out = jnp.einsum('cmnb,kn->bckm', real_in, cosine, precision=HIGHEST) + jnp.einsum('cmnb,kn->bckm', imag_in, sine_table, precision=HIGHEST)
    imag_out = jnp.einsum('cmnb,kn->bckm', imag_in, cosine, precision=HIGHEST) - jnp.einsum('cmnb,kn->bckm', real_in, sine_table, precision=HIGHEST)
    return real_out * real_out + imag_out * imag_out

def dedisperse(normed, slopes, trials, live_total):
    delays = trials[None, :] * slopes[:, None] // (DM - 1)
    initial = jnp.zeros((normed.shape[0], TOUT, trials.shape[0]), jnp.float32)

    def add_delay(delay_step, total_sum):
        delay_index = jnp.asarray(delay_step).astype(jnp.int32)
        window = lax.dynamic_slice_in_dim(normed, delay_index, TOUT, 2).astype(jnp.float32)
        picked = (delays == delay_index).astype(jnp.float32)
        return total_sum + jnp.einsum('bct,cd->btd', window, picked, precision=HIGHEST)
    return lax.fori_loop(0, MAXD + 1, add_delay, initial) / jnp.sqrt(live_total)

def reference(voltages, gains, slopes, mask):
    feed_count = voltages.shape[-1]
    weights = beam_table(feed_count, jnp.arange(BEAMS, dtype=jnp.int32)).astype(jnp.float32)

    def channel(channel_pair):
        voltage, gain_group = channel_pair
        calibrated = calibrate(voltage, gain_group)
        formed = jnp.dot(calibrated.reshape(-1, 2 * feed_count).astype(jnp.float32), weights, precision=HIGHEST)
        formed = formed.astype(jnp.bfloat16).reshape(GROUPS, -1, 2 * BEAMS)
        group_power = fine_power(formed).astype(jnp.bfloat16)
        return lax.optimization_barrier(jnp.sum(group_power.astype(jnp.float32), axis=1)).astype(jnp.bfloat16)
    summed = lax.map(channel, (voltages, gains))
    channel_count = summed.shape[0]
    totals = lax.optimization_barrier(jnp.sum(summed.astype(jnp.float32), axis=(1, 3)))
    channel_mean = totals / (BEAMS * FR)
    live_mask = mask.astype(jnp.float32).reshape(channel_count, 1, UP, 1)
    relative = summed.astype(jnp.float32) / (channel_mean[:, None, :, None] + EPSILON)
    normed = (live_mask * (relative - 1.0)).astype(jnp.bfloat16)
    normed = jnp.transpose(normed, (1, 0, 2, 3)).reshape(BEAMS, channel_count * UP, FR)
    live_total = jnp.sum(mask).astype(jnp.float32)
    trials = jnp.arange(DM, dtype=jnp.int32)
    block_size = min(64, BEAMS)
    stacked = normed.reshape(BEAMS // block_size, block_size, channel_count * UP, FR)
    result = lax.map(lambda beam_block: dedisperse(beam_block, slopes, trials, live_total), stacked)
    return result.reshape(BEAMS, TOUT, DM)
```

```python
import functools
import math

import jax
import jax.numpy as jnp
import ml_dtypes
import numpy as np
from jax import lax
from jax.experimental import pallas as pl
from jax.experimental.pallas import tpu as pltpu
from jax.sharding import PartitionSpec as P

FEEDS = 512
BEAMS = 1024
UP = 16
TAPS = 16
DM = 96
MAXD = 48
TOUT = 24
FR = 72
TS = 1392
POL = 4
FREQ = 128
PAIR = BEAMS // (POL * FREQ)
QUARTER = FREQ * PAIR
MG = 8
BLOCKS = FR // MG
ROWS = UP * MG
SPAN = (MG - 1 + TAPS) * UP
SLOTS = 64
USED = 56
TILES = FEEDS // 128
EPSILON = 1e-06
BF16 = ml_dtypes.bfloat16
VMEM_LIMIT = 48 * 1024 * 1024


@functools.lru_cache(None)
def beam_tables():
    n = np.arange(FEEDS)[:, None]
    f = np.arange(FREQ)[:, None]
    b = np.arange(PAIR)[None, :]
    out = []
    for q in range(POL):
        k = (f * (POL * PAIR) + q * PAIR + b).reshape(1, -1)
        turn = (n * k) % BEAMS
        angle = turn.astype(np.float32) * np.float32(2.0 * math.pi / BEAMS)
        scale = np.float32(1.0 / math.sqrt(FEEDS))
        c = np.cos(angle) * scale
        s = np.sin(angle) * scale
        top = np.concatenate([c, -s], axis=1)
        low = np.concatenate([s, c], axis=1)
        out.append(np.concatenate([top, low], axis=0))
    return np.stack(out).astype(BF16)


@functools.lru_cache(None)
def bank_matrix():
    length = TAPS * UP
    pos = np.arange(length, dtype=np.float64) + 0.5
    hann = 0.5 - 0.5 * np.cos(2.0 * math.pi * pos / length)
    taps = (np.sinc((pos - 0.5 * length) / UP) * hann).astype(np.float32).astype(BF16)
    taps = taps.astype(np.float64)
    real = np.zeros((2, UP, MG, SPAN))
    imag = np.zeros((2, UP, MG, SPAN))
    lag = np.arange(length)
    for u in range(UP):
        angle = 2.0 * math.pi * ((u * lag) % UP) / UP
        c, s = taps * np.cos(angle), taps * np.sin(angle)
        for m in range(MG):
            at = slice(m * UP, m * UP + length)
            real[0, u, m, at], imag[0, u, m, at] = c, s
            real[1, u, m, at], imag[1, u, m, at] = -s, c
    both = np.concatenate([real.reshape(2 * ROWS, SPAN), imag.reshape(2 * ROWS, SPAN)], axis=1)
    return both.astype(np.float32).astype(BF16)


@functools.lru_cache(None)
def fold_matrix():
    g, u, m8 = np.meshgrid(np.arange(BLOCKS), np.arange(UP), np.arange(MG), indexing="ij")
    m = (g * MG + m8).reshape(-1)
    return (m[:, None] == np.arange(128)[None, :]).astype(np.float32).astype(BF16)


def first_slope(delay):
    return 8 * (delay // 8)


@functools.lru_cache(None)
def trial_matrix():
    parts = []
    share = DM // POL
    for delay in range(MAXD + 1):
        slope = np.arange(first_slope(delay), USED)
        block = np.zeros((POL * 32, slope.size), np.float32)
        for d in range(DM):
            block[(d // share) * 32 + d % share] = ((d * slope) // (DM - 1) == delay) & (slope <= MAXD)
        parts.append(block)
    full = np.concatenate(parts, axis=1)
    return full.astype(BF16)


STACK = sum(USED - first_slope(delay) for delay in range(MAXD + 1))


def calibrate_kernel(v_ref, g_ref, out_ref, wide):
    rows = out_ref.shape[0]
    wide[...] = v_ref[...].astype(jnp.float32)
    for j in range(TILES):
        lanes = slice(j * 128, (j + 1) * 128)
        re = wide[pl.ds(2 * j, rows, stride=2 * TILES), :]
        im = wide[pl.ds(2 * j + 1, rows, stride=2 * TILES), :]
        gr = g_ref[0:1, lanes]
        gi = g_ref[1:2, lanes]
        out_ref[:, lanes] = (re * gr - im * gi).astype(jnp.bfloat16)
        out_ref[:, FEEDS + j * 128 : FEEDS + (j + 1) * 128] = (re * gi + im * gr).astype(jnp.bfloat16)


def calibrate(voltages, gains):
    block = 464
    flat = voltages.reshape(TS, 2, TILES, 128).transpose(0, 2, 1, 3).reshape(TS * TILES * 2, 128)
    return pl.pallas_call(
        calibrate_kernel,
        grid=(TS // block,),
        in_specs=[
            pl.BlockSpec((block * 2 * TILES, 128), lambda i: (i, 0)),
            pl.BlockSpec((2, FEEDS), lambda i: (0, 0)),
        ],
        out_specs=pl.BlockSpec((block, 2 * FEEDS), lambda i: (i, 0)),
        out_shape=jax.ShapeDtypeStruct((TS, 2 * FEEDS), jnp.bfloat16),
        scratch_shapes=[pltpu.VMEM((block * 2 * TILES, 128), jnp.float32)],
        compiler_params=pltpu.CompilerParams(vmem_limit_bytes=VMEM_LIMIT),
        name="calibrate",
    )(flat, gains)


def power_kernel(q_ref, cal_ref, tab_ref, bank_ref, out_ref, tot_ref, formed):
    del q_ref
    for i in range(3):
        rows = slice(i * 464, (i + 1) * 464)
        formed[rows, :] = jnp.dot(
            cal_ref[rows, :], tab_ref[...], preferred_element_type=jnp.float32
        ).astype(jnp.bfloat16)
    total = jnp.zeros((ROWS, QUARTER), jnp.float32)
    for g in range(BLOCKS):
        rows = slice(g * ROWS, g * ROWS + SPAN)
        both = jnp.concatenate([formed[rows, :QUARTER], formed[rows, QUARTER:]], axis=0)
        fine = jnp.dot(bank_ref[...], both, preferred_element_type=jnp.float32)
        re, im = fine[:ROWS], fine[ROWS:]
        power = (re * re + im * im).astype(jnp.bfloat16)
        out_ref[g * ROWS : (g + 1) * ROWS, :] = power
        total = total + power.astype(jnp.float32)
    for u in range(UP):
        part = total[u * MG : (u + 1) * MG]
        tot_ref[u : u + 1, :] = jnp.broadcast_to(jnp.sum(part, keepdims=True), (1, 128))


def quarter_power(index, calibrated, tables, bank):
    return pl.pallas_call(
        power_kernel,
        grid_spec=pltpu.PrefetchScalarGridSpec(
            num_scalar_prefetch=1,
            grid=(1,),
            in_specs=[
                pl.BlockSpec((TS, 2 * FEEDS), lambda i, q: (0, 0)),
                pl.BlockSpec((None, 2 * FEEDS, 2 * QUARTER), lambda i, q: (q[0], 0, 0)),
                pl.BlockSpec((2 * ROWS, 2 * SPAN), lambda i, q: (0, 0)),
            ],
            out_specs=[
                pl.BlockSpec((UP * FR, QUARTER), lambda i, q: (0, 0)),
                pl.BlockSpec((UP, 128), lambda i, q: (0, 0)),
            ],
            scratch_shapes=[pltpu.VMEM((TS, 2 * QUARTER), jnp.bfloat16)],
        ),
        out_shape=[
            jax.ShapeDtypeStruct((UP * FR, QUARTER), jnp.bfloat16),
            jax.ShapeDtypeStruct((UP, 128), jnp.float32),
        ],
        compiler_params=pltpu.CompilerParams(vmem_limit_bytes=VMEM_LIMIT),
        cost_estimate=pl.CostEstimate(
            flops=2 * TS * 2 * FEEDS * 2 * QUARTER, bytes_accessed=5_000_000, transcendentals=0
        ),
        name="quarter_power",
    )(index.reshape(1), calibrated, tables, bank)


def normalize_kernel(tot_ref, a_ref, b_ref, c_ref, d_ref, out_ref, inverse):
    for u in range(UP):
        mean = tot_ref[u : u + 1, :] * (1.0 / (BEAMS * FR))
        inverse[u * MG : (u + 1) * MG, :] = jnp.broadcast_to(1.0 / (mean + EPSILON), (MG, 128))
    scale = jnp.concatenate([inverse[...]] * (QUARTER // 128), axis=1)
    for g in range(BLOCKS):
        rows = slice(g * ROWS, (g + 1) * ROWS)
        total = a_ref[rows, :].astype(jnp.float32) + b_ref[rows, :].astype(jnp.float32)
        total = total + c_ref[rows, :].astype(jnp.float32) + d_ref[rows, :].astype(jnp.float32)
        summed = total.astype(jnp.bfloat16).astype(jnp.float32)
        normed = summed * scale - 1.0
        out_ref[:, rows] = normed.T.astype(jnp.bfloat16)


def normalize(totals, parts):
    return pl.pallas_call(
        normalize_kernel,
        out_shape=jax.ShapeDtypeStruct((QUARTER, UP * FR), jnp.bfloat16),
        scratch_shapes=[pltpu.VMEM((ROWS, 128), jnp.float32)],
        compiler_params=pltpu.CompilerParams(vmem_limit_bytes=VMEM_LIMIT),
        name="normalize",
    )(totals, *parts)


def dedisperse_kernel(scale_ref, x_ref, hot_ref, fold_ref, trial_ref, out_ref, by_slope, stack):
    for at in range(0, UP * FR, 256):
        width = min(256, UP * FR - at)
        product = jnp.dot(hot_ref[...], x_ref[:, at : at + width], preferred_element_type=jnp.float32)
        lane = lax.broadcasted_iota(jnp.int32, (PAIR * SLOTS, width), 1)
        fine = lane // MG % UP
        total = jnp.zeros((PAIR * SLOTS, width), jnp.float32)
        for u in range(UP):
            rows = slice(u * PAIR * SLOTS, (u + 1) * PAIR * SLOTS)
            total = jnp.where(fine == u, product[rows, :], total)
        by_slope[:, at : at + width] = total
    whole = by_slope[...]
    high = whole.astype(jnp.bfloat16)
    low = (whole - high.astype(jnp.float32)).astype(jnp.bfloat16)
    series = jnp.dot(high, fold_ref[...], preferred_element_type=jnp.float32)
    series = series + jnp.dot(low, fold_ref[...], preferred_element_type=jnp.float32)
    at = 0
    for delay in range(MAXD + 1):
        first = first_slope(delay)
        size = USED - first
        for b in range(PAIR):
            rows = series[b * SLOTS + first : b * SLOTS + USED, :]
            if delay:
                rows = pltpu.roll(rows, 128 - delay, 1)
            stack[at : at + size, b * 128 : (b + 1) * 128] = rows
        at += size
    shifted = stack[...]
    high = shifted.astype(jnp.bfloat16)
    low = (shifted - high.astype(jnp.float32)).astype(jnp.bfloat16)
    series = jnp.dot(trial_ref[...], high, preferred_element_type=jnp.float32)
    series = series + jnp.dot(trial_ref[...], low, preferred_element_type=jnp.float32)
    series = series * scale_ref[0, 0]
    share = DM // POL
    for b in range(PAIR):
        turned = series[:, b * 128 : (b + 1) * 128].T
        for q in range(POL):
            out_ref[q, b] = turned[:TOUT, q * 32 : q * 32 + share]


def dedisperse(scale, normed, hot):
    vmem = pl.BlockSpec(memory_space=pltpu.VMEM)
    return pl.pallas_call(
        dedisperse_kernel,
        in_specs=[pl.BlockSpec(memory_space=pltpu.SMEM), vmem, vmem, vmem, vmem],
        out_specs=vmem,
        out_shape=jax.ShapeDtypeStruct((POL, PAIR, TOUT, DM // POL), jnp.float32),
        scratch_shapes=[
            pltpu.VMEM((PAIR * SLOTS, UP * FR), jnp.float32),
            pltpu.VMEM((STACK, PAIR * 128), jnp.float32),
        ],
        compiler_params=pltpu.CompilerParams(vmem_limit_bytes=VMEM_LIMIT),
        name="dedisperse",
    )(scale, normed, hot, jnp.asarray(fold_matrix()), jnp.asarray(trial_matrix()))


def slope_picker(slopes, mask):
    marked = jnp.where(mask != 0, slopes, -1).reshape(FREQ, UP).T
    marked = jnp.repeat(marked, PAIR, axis=1)[:, None, None, :]
    slope = jnp.arange(SLOTS, dtype=jnp.int32)[None, None, :, None]
    beam = jnp.arange(PAIR, dtype=jnp.int32)[None, :, None, None]
    column = jnp.arange(QUARTER, dtype=jnp.int32)[None, None, None, :]
    hot = (marked == slope) & (column % PAIR == beam)
    return hot.astype(jnp.bfloat16).reshape(UP * PAIR * SLOTS, QUARTER)


def on_device(voltages, gains, slopes, mask):
    me = lax.axis_index("pol")
    calibrated = calibrate(voltages[0, 0], gains[0, 0])
    tables = jnp.asarray(beam_tables())
    bank = jnp.asarray(bank_matrix())
    parts = []
    totals = 0.0
    for ahead in (2, 1, 3, 0):
        power, total = quarter_power((me + ahead) % POL, calibrated, tables, bank)
        totals = totals + total
        if ahead:
            power = lax.ppermute(power, "pol", [(i, (i + ahead) % POL) for i in range(POL)])
        parts.append(power)
    totals = lax.psum(totals, "pol")
    normed = normalize(totals, parts)
    turned = lax.all_to_all(normed.reshape(FREQ, PAIR, UP * FR), "freq", 0, 0, tiled=True)
    scale = lax.rsqrt(jnp.sum(mask).astype(jnp.float32)).reshape(1, 1)
    out = dedisperse(scale, turned.reshape(QUARTER, UP * FR), slope_picker(slopes, mask))
    out = lax.all_to_all(out, "pol", 0, 0, tiled=True)
    return out.reshape(POL * PAIR, TOUT, DM // POL)


def solution(mesh):
    placed = (P("freq", "pol", None, None, None), P("freq", "pol", None, None), P(), P())
    return jax.shard_map(
        on_device, mesh=mesh, in_specs=placed, out_specs=P("freq", None, "pol"), check_vma=False
    )
```

```python
import functools
import math

import jax
import jax.numpy as jnp
import ml_dtypes
import numpy as np
from jax import lax
from jax.experimental import pallas as pl
from jax.experimental.pallas import tpu as pltpu
from jax.sharding import PartitionSpec as P

FEEDS = 512
BEAMS = 1024
UP = 16
TAPS = 16
DM = 96
MAXD = 48
TOUT = 24
FR = 72
TS = 1392
POL = 4
FREQ = 128
PAIR = BEAMS // (POL * FREQ)
QUARTER = FREQ * PAIR
MG = 8
BLOCKS = FR // MG
ROWS = UP * MG
SPAN = (MG - 1 + TAPS) * UP
SLOTS = 56
TILES = FEEDS // 128
KINDS = 2 * TILES
CHUNKS = ((0, 368), (368, 512), (880, 512))
CORES = 2
CHIPS = FREQ // CORES
HELD = CORES * PAIR
EPSILON = 1e-06
BF16 = ml_dtypes.bfloat16
VMEM_LIMIT = 32 * 1024 * 1024
WHOLE_VMEM = 58 * 1024 * 1024


@functools.lru_cache(None)
def beam_tables():
    n = np.arange(FEEDS)[:, None]
    f = np.arange(FREQ)[None, :]
    b = np.arange(PAIR)[:, None]
    scale = np.float32(1.0 / math.sqrt(FEEDS))
    out = []
    for q in range(POL):
        k = (f * (POL * PAIR) + q * PAIR + b).reshape(1, -1)
        angle = ((n * k) % BEAMS).astype(np.float32) * np.float32(2.0 * math.pi / BEAMS)
        c = np.cos(angle) * scale
        s = np.sin(angle) * scale
        top = np.concatenate([c, -s], axis=1)
        low = np.concatenate([s, c], axis=1)
        out.append(np.concatenate([top, low], axis=0))
    return np.stack(out).astype(BF16)


@functools.lru_cache(None)
def bank_matrix():
    length = TAPS * UP
    pos = np.arange(length, dtype=np.float64) + 0.5
    hann = 0.5 - 0.5 * np.cos(2.0 * math.pi * pos / length)
    taps = (np.sinc((pos - 0.5 * length) / UP) * hann).astype(np.float32).astype(BF16)
    taps = taps.astype(np.float64)
    real = np.zeros((2, UP, MG, SPAN))
    imag = np.zeros((2, UP, MG, SPAN))
    lag = np.arange(length)
    for u in range(UP):
        angle = 2.0 * math.pi * ((u * lag) % UP) / UP
        c, s = taps * np.cos(angle), taps * np.sin(angle)
        for m in range(MG):
            at = slice(m * UP, m * UP + length)
            real[0, u, m, at], imag[0, u, m, at] = c, s
            real[1, u, m, at], imag[1, u, m, at] = -s, c
    both = np.concatenate([real.reshape(2 * ROWS, SPAN), imag.reshape(2 * ROWS, SPAN)], axis=1)
    return both.astype(np.float32).astype(BF16)


@functools.lru_cache(None)
def fold_matrix():
    g, u, m8 = np.meshgrid(np.arange(BLOCKS), np.arange(UP), np.arange(MG), indexing="ij")
    m = (g * MG + m8).reshape(-1)
    return (m[:, None] == np.arange(128)[None, :]).astype(np.float32).astype(BF16)


def first_slope(delay):
    return 8 * (delay // 8)


@functools.lru_cache(None)
def trial_matrix():
    parts = []
    share = DM // POL
    for delay in range(MAXD + 1):
        slope = np.arange(first_slope(delay), SLOTS)
        block = np.zeros((POL * 32, slope.size), np.float32)
        for d in range(DM):
            block[(d // share) * 32 + d % share] = ((d * slope) // (DM - 1) == delay) & (slope <= MAXD)
        parts.append(block)
    full = np.concatenate(parts, axis=1)
    return full.astype(BF16)


STACK = sum(SLOTS - first_slope(delay) for delay in range(MAXD + 1))


VMEM = pl.BlockSpec(memory_space=pltpu.VMEM)
SMEM = pl.BlockSpec(memory_space=pltpu.SMEM)
HBM = pl.BlockSpec(memory_space=pltpu.HBM)
PARAMS = pltpu.CompilerParams(vmem_limit_bytes=VMEM_LIMIT)
WHOLE = pltpu.CompilerParams(vmem_limit_bytes=WHOLE_VMEM)


def by_kind(block):
    samples = block.shape[0] // KINDS
    lifted = block.reshape(samples // 8, 8, KINDS, 128)
    parts = [lifted[:, t] for t in range(8)]
    row = lax.broadcasted_iota(jnp.int32, parts[0].shape, 1)
    for bit in (1, 2, 4):
        low = (row & bit) == 0
        for t in range(8):
            if t & bit == 0:
                a, b = parts[t], parts[t + bit]
                parts[t] = jnp.where(low, a, pltpu.roll(b, bit, 1))
                parts[t + bit] = jnp.where(low, pltpu.roll(a, 8 - bit, 1), b)
    return [part.reshape(samples, 128) for part in parts]


def calibrate_rows(v_ref, g_ref, cal_ref, start, size):
    kinds = by_kind(v_ref[start * KINDS : (start + size) * KINDS, :].astype(jnp.float32))
    rows = slice(start, start + size)
    for j in range(TILES):
        re, im = kinds[2 * j], kinds[2 * j + 1]
        lanes = slice(j * 128, (j + 1) * 128)
        gr = g_ref[0:1, lanes]
        gi = g_ref[1:2, lanes]
        cal_ref[rows, lanes] = (re * gr - im * gi).astype(jnp.bfloat16)
        lanes = slice(FEEDS + j * 128, FEEDS + (j + 1) * 128)
        cal_ref[rows, lanes] = (re * gi + im * gr).astype(jnp.bfloat16)


def form(cal_ref, tab_ref, formed, start, size):
    rows = slice(start, start + size)
    formed[rows, :] = jnp.dot(
        cal_ref[rows, :], tab_ref[...], preferred_element_type=jnp.float32
    ).astype(jnp.bfloat16)


def filter_power(bank_ref, formed, out_ref, tot_ref):
    total = jnp.zeros((ROWS, QUARTER), jnp.float32)
    for g in range(BLOCKS):
        rows = slice(g * ROWS, g * ROWS + SPAN)
        both = jnp.concatenate([formed[rows, :QUARTER], formed[rows, QUARTER:]], axis=0)
        fine = jnp.dot(bank_ref[...], both, preferred_element_type=jnp.float32)
        re, im = fine[:ROWS], fine[ROWS:]
        power = (re * re + im * im).astype(jnp.bfloat16)
        out_ref[g * ROWS : (g + 1) * ROWS, :] = power
        total = total + power.astype(jnp.float32)
    for u in range(UP):
        part = total[u * MG : (u + 1) * MG]
        tot_ref[u : u + 1, :] = jnp.broadcast_to(jnp.sum(part, keepdims=True), (1, 128))


def row_copies(source, target, sems, scale=1):
    copies = []
    for i, (start, size) in enumerate(CHUNKS):
        rows = pl.ds(start * scale, size * scale)
        copies.append(pltpu.make_async_copy(source.at[rows, :], target.at[rows, :], sems.at[i]))
    return copies


def lead_kernel(
    q_ref, v_hbm, g_ref, tab_hbm, bank_ref, out_ref, tot_ref, cal_hbm, v_ref, tab_ref, cal_ref, formed, sems
):
    loads = row_copies(v_hbm, v_ref, sems.at[0], KINDS)
    stores = row_copies(cal_ref, cal_hbm, sems.at[1])
    table = pltpu.make_async_copy(tab_hbm.at[q_ref[0]], tab_ref, sems.at[2, 0])
    for copy in loads[:1] + [table] + loads[1:]:
        copy.start()
    for i in range(len(CHUNKS) + 1):
        if i < len(CHUNKS):
            loads[i].wait()
            calibrate_rows(v_ref, g_ref, cal_ref, *CHUNKS[i])
            stores[i].start()
        if i == 0:
            table.wait()
        else:
            form(cal_ref, tab_ref, formed, *CHUNKS[i - 1])
    filter_power(bank_ref, formed, out_ref, tot_ref)
    for copy in stores:
        copy.wait()


REST = POL - 1


def rest_kernel(q_ref, cal_hbm, tab_hbm, bank_ref, *refs):
    out_hbms, tot_ref = refs[:REST], refs[REST]
    cal_ref, tab_ref, formed, out_ref, tot_parts, cal_sems, tab_sems, out_sems = refs[REST + 1 :]
    loads = row_copies(cal_hbm, cal_ref, cal_sems)
    tables = [
        pltpu.make_async_copy(tab_hbm.at[q_ref[n]], tab_ref.at[n], tab_sems.at[n]) for n in range(REST)
    ]
    for copy in tables[:1] + loads + tables[1:]:
        copy.start()
    stores = []
    for n in range(REST):
        tables[n].wait()
        for i, chunk in enumerate(CHUNKS):
            if n == 0:
                loads[i].wait()
            form(cal_ref, tab_ref.at[n], formed.at[n], *chunk)
        filter_power(bank_ref, formed.at[n], out_ref.at[n], tot_parts.at[n])
        stores.append(pltpu.make_async_copy(out_ref.at[n], out_hbms[n], out_sems.at[n]))
        stores[-1].start()
    tot_ref[...] = tot_parts[0] + tot_parts[1] + tot_parts[2]
    for copy in stores:
        copy.wait()


POWER = jax.ShapeDtypeStruct((UP * FR, QUARTER), jnp.bfloat16)
TOTAL = jax.ShapeDtypeStruct((UP, 128), jnp.float32)
def lead_power(index, voltages, gains, tables, bank):
    flat = voltages.reshape(TS, 2, TILES, 128).transpose(0, 2, 1, 3).reshape(TS * KINDS, 128)
    return pl.pallas_call(
        lead_kernel,
        in_specs=[SMEM, HBM, VMEM, HBM, VMEM],
        out_specs=[VMEM, VMEM, HBM],
        out_shape=[POWER, TOTAL, jax.ShapeDtypeStruct((TS, 2 * FEEDS), jnp.bfloat16)],
        scratch_shapes=[
            pltpu.VMEM((TS * KINDS, 128), jnp.bfloat16),
            pltpu.VMEM((2 * FEEDS, 2 * QUARTER), jnp.bfloat16),
            pltpu.VMEM((TS, 2 * FEEDS), jnp.bfloat16),
            pltpu.VMEM((TS, 2 * QUARTER), jnp.bfloat16),
            pltpu.SemaphoreType.DMA((3, len(CHUNKS))),
        ],
        compiler_params=WHOLE,
        cost_estimate=pl.CostEstimate(flops=3_000_000_000, bytes_accessed=8_000_000, transcendentals=0),
        name="lead_power",
    )(index.reshape(1), flat, gains, tables, bank)


def rest_powers(indices, calibrated, tables, bank):
    return pl.pallas_call(
        rest_kernel,
        in_specs=[SMEM, HBM, HBM, VMEM],
        out_specs=[HBM] * REST + [VMEM],
        out_shape=[POWER] * REST + [TOTAL],
        scratch_shapes=[
            pltpu.VMEM((TS, 2 * FEEDS), jnp.bfloat16),
            pltpu.VMEM((REST, 2 * FEEDS, 2 * QUARTER), jnp.bfloat16),
            pltpu.VMEM((REST, TS, 2 * QUARTER), jnp.bfloat16),
            pltpu.VMEM((REST, UP * FR, QUARTER), jnp.bfloat16),
            pltpu.VMEM((REST, UP, 128), jnp.float32),
            pltpu.SemaphoreType.DMA((len(CHUNKS),)),
            pltpu.SemaphoreType.DMA((REST,)),
            pltpu.SemaphoreType.DMA((REST,)),
        ],
        compiler_params=WHOLE,
        cost_estimate=pl.CostEstimate(flops=9_000_000_000, bytes_accessed=8_000_000, transcendentals=0),
        name="rest_powers",
    )(jnp.stack(indices), calibrated, tables, bank)


def normalize_kernel(tot_ref, a_ref, b_ref, c_ref, d_ref, out_ref, inverse):
    for u in range(UP):
        mean = tot_ref[u : u + 1, :] * (1.0 / (BEAMS * FR))
        inverse[u * MG : (u + 1) * MG, :] = jnp.broadcast_to(1.0 / (mean + EPSILON), (MG, 128))
    scale = inverse[...]
    for g in range(BLOCKS):
        rows = slice(g * ROWS, (g + 1) * ROWS)
        for b in range(PAIR):
            lanes = slice(b * FREQ, (b + 1) * FREQ)
            total = d_ref[rows, lanes].astype(jnp.float32)
            for ref in (a_ref, b_ref, c_ref):
                total = total + ref[rows, lanes].astype(jnp.float32)
            summed = total.astype(jnp.bfloat16).astype(jnp.float32)
            normed = summed * scale - 1.0
            at = b * UP * FR + g * ROWS
            out_ref[:, at : at + ROWS] = normed.T.astype(jnp.bfloat16)


def normalize(totals, parts):
    return pl.pallas_call(
        normalize_kernel,
        in_specs=[VMEM] * (1 + POL),
        out_specs=VMEM,
        out_shape=jax.ShapeDtypeStruct((FREQ, PAIR * UP * FR), jnp.bfloat16),
        scratch_shapes=[pltpu.VMEM((ROWS, 128), jnp.float32)],
        compiler_params=PARAMS,
        name="normalize",
    )(totals, *parts)


def dedisperse_kernel(scale_ref, x_ref, hot_ref, fold_ref, trial_ref, out_ref, by_slope, stack):
    picked = CORES * SLOTS
    series = [None] * HELD
    for b in range(PAIR):
        for at in range(0, UP * FR, 256):
            width = min(256, UP * FR - at)
            start = b * UP * FR + at
            values = x_ref[:, start : start + width]
            fine = lax.broadcasted_iota(jnp.int32, values.shape, 1) // MG
            empty = jnp.zeros_like(values)
            even = jnp.where(fine % 2 == 0, values, empty)
            odd = jnp.where(fine % 2 == 0, empty, values)
            both = jnp.concatenate([even, odd], axis=0)
            product = jnp.dot(hot_ref[...], both, preferred_element_type=jnp.float32)
            couple = lax.broadcasted_iota(jnp.int32, (picked, width), 1) // (2 * MG) % (UP // 2)
            total = product[:picked, :]
            for n in range(1, UP // 2):
                total = jnp.where(couple == n, product[n * picked : (n + 1) * picked, :], total)
            by_slope[b, :, at : at + width] = total
        whole = by_slope[b]
        high = whole.astype(jnp.bfloat16)
        low = (whole - high.astype(jnp.float32)).astype(jnp.bfloat16)
        folded = jnp.dot(high, fold_ref[...], preferred_element_type=jnp.float32)
        folded = folded + jnp.dot(low, fold_ref[...], preferred_element_type=jnp.float32)
        for core in range(CORES):
            series[core * PAIR + b] = folded[core * SLOTS : (core + 1) * SLOTS]
    lane = lax.broadcasted_iota(jnp.int32, (SLOTS, 128), 1) // 32
    at = 0
    for delay in range(MAXD + 1):
        first = first_slope(delay)
        size = SLOTS - first
        packed = jnp.zeros((size, 128), jnp.float32)
        for b in range(HELD):
            rows = series[b][first:, :]
            shift = (32 * b - delay) % 128
            rows = pltpu.roll(rows, shift, 1) if shift else rows
            packed = jnp.where(lane[:size] == b, rows, packed)
        stack[at : at + size, :] = packed
        at += size
    shifted = stack[...]
    high = shifted.astype(jnp.bfloat16)
    low = (shifted - high.astype(jnp.float32)).astype(jnp.bfloat16)
    result = jnp.dot(trial_ref[...], high, preferred_element_type=jnp.float32)
    result = result + jnp.dot(trial_ref[...], low, preferred_element_type=jnp.float32)
    turned = (result * scale_ref[0, 0]).T
    for q in range(POL):
        rolled = pltpu.roll(turned, 128 - 32 * q, 1) if q else turned
        for core in range(CORES):
            for b in range(PAIR):
                start = 32 * (core * PAIR + b)
                out_ref[core * POL + q, b] = rolled[start : start + TOUT]


def dedisperse(scale, normed, hot):
    return pl.pallas_call(
        dedisperse_kernel,
        in_specs=[SMEM, VMEM, VMEM, VMEM, VMEM],
        out_specs=VMEM,
        out_shape=jax.ShapeDtypeStruct((CORES * POL, PAIR, TOUT, 128), jnp.float32),
        scratch_shapes=[
            pltpu.VMEM((PAIR, CORES * SLOTS, UP * FR), jnp.float32),
            pltpu.VMEM((STACK, 128), jnp.float32),
        ],
        compiler_params=PARAMS,
        name="dedisperse",
    )(scale, normed, hot, jnp.asarray(fold_matrix()), jnp.asarray(trial_matrix()))


def slope_picker(slopes, mask, core):
    marked = jnp.where(mask != 0, slopes, -1).reshape(CHIPS, CORES, UP)
    marked = lax.dynamic_index_in_dim(marked, core, 1, keepdims=False).T.reshape(UP // 2, 2 * CHIPS)
    marked = jnp.repeat(marked, CORES, axis=1)[:, None, None, :]
    slope = jnp.arange(SLOTS, dtype=jnp.int32)[None, None, :, None]
    own = jnp.arange(CORES, dtype=jnp.int32)[None, :, None, None]
    column = jnp.arange(2 * FREQ, dtype=jnp.int32)[None, None, None, :]
    hot = (marked == slope) & (column % CORES == own)
    return hot.astype(jnp.bfloat16).reshape(UP // 2 * CORES * SLOTS, 2 * FREQ)


def on_device(voltages, gains, slopes, mask):
    me = lax.axis_index("pol")
    core = lax.axis_index("freq") % CORES
    tables = jnp.asarray(beam_tables())
    bank = jnp.asarray(bank_matrix())
    index = [(me + ahead) % POL for ahead in range(POL)]

    def send(power, ahead):
        return lax.ppermute(power, "pol", [(i, (i + ahead) % POL) for i in range(POL)])

    far, far_total, calibrated = lead_power(index[2], voltages[0, 0], gains[0, 0], tables, bank)
    far = send(far, 2)
    right, left, own, rest_total = rest_powers([index[1], index[3], index[0]], calibrated, tables, bank)
    parts = [far, send(right, 1), send(left, 3), own]
    normed = normalize(lax.psum(far_total + rest_total, "pol"), parts)
    alike = [[CORES * chip + c for chip in range(CHIPS)] for c in range(CORES)]
    turned = lax.all_to_all(
        normed.reshape(CHIPS, CORES, PAIR * UP * FR), "freq", 0, 0, tiled=True, axis_index_groups=alike
    )
    scale = lax.rsqrt(jnp.sum(mask).astype(jnp.float32)).reshape(1, 1)
    out = dedisperse(scale, turned.reshape(FREQ, PAIR * UP * FR), slope_picker(slopes, mask, core))
    near = [
        [(CORES * chip + c) * POL + q for c in range(CORES) for q in range(POL)] for chip in range(CHIPS)
    ]
    out = lax.all_to_all(out, ("freq", "pol"), 0, 0, tiled=True, axis_index_groups=near)
    out = out[:POL] + out[POL:]
    return out.reshape(POL * PAIR, TOUT, 128)[:, :, : DM // POL]


def solution(mesh):
    placed = (P("freq", "pol", None, None, None), P("freq", "pol", None, None), P(), P())
    return jax.shard_map(
        on_device, mesh=mesh, in_specs=placed, out_specs=P("freq", None, "pol"), check_vma=False
    )
```

```python
import functools
import math

import jax
import jax.numpy as jnp
import ml_dtypes
import numpy as np
from jax import lax
from jax.experimental import pallas as pl
from jax.experimental.pallas import tpu as pltpu
from jax.sharding import PartitionSpec as P

FEEDS = 512
BEAMS = 1024
UP = 16
TAPS = 16
DM = 96
MAXD = 48
TOUT = 24
FR = 72
TS = 1392
POL = 4
FREQ = 128
PAIR = BEAMS // (POL * FREQ)
QUARTER = FREQ * PAIR
MG = 8
BLOCKS = FR // MG
ROWS = UP * MG
SPAN = (MG - 1 + TAPS) * UP
SLOTS = 56
TILES = FEEDS // 128
KINDS = 2 * TILES
CHUNKS = ((0, 464), (464, 464), (928, 464))
CORES = 2
CHIPS = FREQ // CORES
HELD = CORES * PAIR
EPSILON = 1e-06
BF16 = ml_dtypes.bfloat16
VMEM_LIMIT = 32 * 1024 * 1024
WHOLE_VMEM = 48 * 1024 * 1024


@functools.lru_cache(None)
def beam_tables():
    n = np.arange(FEEDS)[:, None]
    f = np.arange(FREQ)[None, :]
    b = np.arange(PAIR)[:, None]
    scale = np.float32(1.0 / math.sqrt(FEEDS))
    out = []
    for q in range(POL):
        k = (f * (POL * PAIR) + q * PAIR + b).reshape(1, -1)
        angle = ((n * k) % BEAMS).astype(np.float32) * np.float32(2.0 * math.pi / BEAMS)
        c = np.cos(angle) * scale
        s = np.sin(angle) * scale
        top = np.concatenate([c, -s], axis=1)
        low = np.concatenate([s, c], axis=1)
        out.append(np.concatenate([top, low], axis=0))
    return np.stack(out).astype(BF16)


@functools.lru_cache(None)
def bank_matrix():
    length = TAPS * UP
    pos = np.arange(length, dtype=np.float64) + 0.5
    hann = 0.5 - 0.5 * np.cos(2.0 * math.pi * pos / length)
    taps = (np.sinc((pos - 0.5 * length) / UP) * hann).astype(np.float32).astype(BF16)
    taps = taps.astype(np.float64)
    real = np.zeros((2, UP, MG, SPAN))
    imag = np.zeros((2, UP, MG, SPAN))
    lag = np.arange(length)
    for u in range(UP):
        angle = 2.0 * math.pi * ((u * lag) % UP) / UP
        c, s = taps * np.cos(angle), taps * np.sin(angle)
        for m in range(MG):
            at = slice(m * UP, m * UP + length)
            real[0, u, m, at], imag[0, u, m, at] = c, s
            real[1, u, m, at], imag[1, u, m, at] = -s, c
    both = np.concatenate([real.reshape(2 * ROWS, SPAN), imag.reshape(2 * ROWS, SPAN)], axis=1)
    return both.astype(np.float32).astype(BF16)


@functools.lru_cache(None)
def fold_matrix():
    g, u, m8 = np.meshgrid(np.arange(BLOCKS), np.arange(UP), np.arange(MG), indexing="ij")
    m = (g * MG + m8).reshape(-1)
    return (m[:, None] == np.arange(128)[None, :]).astype(np.float32).astype(BF16)


def first_slope(delay):
    return 8 * (delay // 8)


@functools.lru_cache(None)
def trial_matrix():
    parts = []
    share = DM // POL
    for delay in range(MAXD + 1):
        slope = np.arange(first_slope(delay), SLOTS)
        block = np.zeros((POL * 32, slope.size), np.float32)
        for d in range(DM):
            block[(d // share) * 32 + d % share] = ((d * slope) // (DM - 1) == delay) & (slope <= MAXD)
        parts.append(block)
    full = np.concatenate(parts, axis=1)
    return full.astype(BF16)


STACK = sum(SLOTS - first_slope(delay) for delay in range(MAXD + 1))


VMEM = pl.BlockSpec(memory_space=pltpu.VMEM)
SMEM = pl.BlockSpec(memory_space=pltpu.SMEM)
HBM = pl.BlockSpec(memory_space=pltpu.HBM)
PARAMS = pltpu.CompilerParams(vmem_limit_bytes=VMEM_LIMIT)
WHOLE = pltpu.CompilerParams(vmem_limit_bytes=WHOLE_VMEM)


def by_kind(block):
    samples = block.shape[0] // KINDS
    lifted = block.reshape(samples // 8, 8, KINDS, 128)
    parts = [lifted[:, t] for t in range(8)]
    row = lax.broadcasted_iota(jnp.int32, parts[0].shape, 1)
    for bit in (1, 2, 4):
        low = (row & bit) == 0
        for t in range(8):
            if t & bit == 0:
                a, b = parts[t], parts[t + bit]
                parts[t] = jnp.where(low, a, pltpu.roll(b, bit, 1))
                parts[t + bit] = jnp.where(low, pltpu.roll(a, 8 - bit, 1), b)
    return [part.reshape(samples, 128) for part in parts]


def calibrate_rows(v_ref, g_ref, cal_ref, start, size):
    kinds = by_kind(v_ref[start * KINDS : (start + size) * KINDS, :].astype(jnp.float32))
    rows = slice(start, start + size)
    for j in range(TILES):
        re, im = kinds[2 * j], kinds[2 * j + 1]
        lanes = slice(j * 128, (j + 1) * 128)
        gr = g_ref[0:1, lanes]
        gi = g_ref[1:2, lanes]
        cal_ref[rows, lanes] = (re * gr - im * gi).astype(jnp.bfloat16)
        lanes = slice(FEEDS + j * 128, FEEDS + (j + 1) * 128)
        cal_ref[rows, lanes] = (re * gi + im * gr).astype(jnp.bfloat16)


def form(cal_ref, tab_ref, formed, start, size):
    rows = slice(start, start + size)
    formed[rows, :] = jnp.dot(
        cal_ref[rows, :], tab_ref[...], preferred_element_type=jnp.float32
    ).astype(jnp.bfloat16)


def filter_power(bank_ref, formed, out_ref, tot_ref):
    total = jnp.zeros((ROWS, QUARTER), jnp.float32)
    for g in range(BLOCKS):
        rows = slice(g * ROWS, g * ROWS + SPAN)
        both = jnp.concatenate([formed[rows, :QUARTER], formed[rows, QUARTER:]], axis=0)
        fine = jnp.dot(bank_ref[...], both, preferred_element_type=jnp.float32)
        re, im = fine[:ROWS], fine[ROWS:]
        power = (re * re + im * im).astype(jnp.bfloat16)
        out_ref[g * ROWS : (g + 1) * ROWS, :] = power
        total = total + power.astype(jnp.float32)
    for u in range(UP):
        part = total[u * MG : (u + 1) * MG]
        tot_ref[u : u + 1, :] = jnp.broadcast_to(jnp.sum(part, keepdims=True), (1, 128))


def calibrate_kernel(v_ref, g_ref, cal_ref):
    for chunk in CHUNKS:
        calibrate_rows(v_ref, g_ref, cal_ref, *chunk)


def power_kernel(count, q_ref, cal_ref, tab_hbm, bank_ref, *refs):
    out_refs, tot_ref = refs[:count], refs[count]
    tab_ref, formed, tot_parts, tab_sems = refs[count + 1 :]
    tables = [
        pltpu.make_async_copy(tab_hbm.at[q_ref[n]], tab_ref.at[n], tab_sems.at[n]) for n in range(count)
    ]
    for copy in tables:
        copy.start()
    for n in range(count):
        tables[n].wait()
        for chunk in CHUNKS:
            form(cal_ref, tab_ref.at[n], formed.at[n], *chunk)
        filter_power(bank_ref, formed.at[n], out_refs[n], tot_parts.at[n])
    total = tot_parts[0]
    for n in range(1, count):
        total = total + tot_parts[n]
    tot_ref[...] = total


BRIEF = pl.CostEstimate(flops=100_000_000, bytes_accessed=10_000, transcendentals=0)
POWER = jax.ShapeDtypeStruct((UP * FR, QUARTER), jnp.bfloat16)
TOTAL = jax.ShapeDtypeStruct((UP, 128), jnp.float32)
def calibrate(voltages, gains):
    flat = voltages.reshape(TS, 2, TILES, 128).transpose(0, 2, 1, 3).reshape(TS * KINDS, 128)
    return pl.pallas_call(
        calibrate_kernel,
        in_specs=[VMEM, VMEM],
        out_specs=VMEM,
        out_shape=jax.ShapeDtypeStruct((TS, 2 * FEEDS), jnp.bfloat16),
        compiler_params=PARAMS,
        name="calibrate",
    )(flat, gains)


def quarter_powers(indices, calibrated, tables, bank):
    count = len(indices)
    return pl.pallas_call(
        functools.partial(power_kernel, count),
        in_specs=[SMEM, VMEM, HBM, VMEM],
        out_specs=[VMEM] * (count + 1),
        out_shape=[POWER] * count + [TOTAL],
        scratch_shapes=[
            pltpu.VMEM((count, 2 * FEEDS, 2 * QUARTER), jnp.bfloat16),
            pltpu.VMEM((count, TS, 2 * QUARTER), jnp.bfloat16),
            pltpu.VMEM((count, UP, 128), jnp.float32),
            pltpu.SemaphoreType.DMA((count,)),
        ],
        compiler_params=WHOLE,
        cost_estimate=BRIEF,
        name="quarter_powers",
    )(jnp.stack(indices), calibrated, tables, bank)


def normalize_kernel(tot_ref, a_ref, b_ref, c_ref, d_ref, out_ref, inverse):
    for u in range(UP):
        mean = tot_ref[u : u + 1, :] * (1.0 / (BEAMS * FR))
        inverse[u * MG : (u + 1) * MG, :] = jnp.broadcast_to(1.0 / (mean + EPSILON), (MG, 128))
    scale = inverse[...]
    for g in range(BLOCKS):
        rows = slice(g * ROWS, (g + 1) * ROWS)
        for b in range(PAIR):
            lanes = slice(b * FREQ, (b + 1) * FREQ)
            total = d_ref[rows, lanes].astype(jnp.float32)
            for ref in (a_ref, b_ref, c_ref):
                total = total + ref[rows, lanes].astype(jnp.float32)
            summed = total.astype(jnp.bfloat16).astype(jnp.float32)
            normed = summed * scale - 1.0
            at = b * UP * FR + g * ROWS
            out_ref[:, at : at + ROWS] = normed.T.astype(jnp.bfloat16)


def normalize(totals, parts):
    return pl.pallas_call(
        normalize_kernel,
        in_specs=[VMEM] * (1 + POL),
        out_specs=VMEM,
        out_shape=jax.ShapeDtypeStruct((FREQ, PAIR * UP * FR), jnp.bfloat16),
        scratch_shapes=[pltpu.VMEM((ROWS, 128), jnp.float32)],
        compiler_params=PARAMS,
        name="normalize",
    )(totals, *parts)


def dedisperse_kernel(scale_ref, x_ref, hot_ref, fold_ref, trial_ref, out_ref, by_slope, stack):
    picked = CORES * SLOTS
    series = [None] * HELD
    for b in range(PAIR):
        for at in range(0, UP * FR, 256):
            width = min(256, UP * FR - at)
            start = b * UP * FR + at
            values = x_ref[:, start : start + width]
            fine = lax.broadcasted_iota(jnp.int32, values.shape, 1) // MG
            empty = jnp.zeros_like(values)
            even = jnp.where(fine % 2 == 0, values, empty)
            odd = jnp.where(fine % 2 == 0, empty, values)
            both = jnp.concatenate([even, odd], axis=0)
            product = jnp.dot(hot_ref[...], both, preferred_element_type=jnp.float32)
            couple = lax.broadcasted_iota(jnp.int32, (picked, width), 1) // (2 * MG) % (UP // 2)
            total = product[:picked, :]
            for n in range(1, UP // 2):
                total = jnp.where(couple == n, product[n * picked : (n + 1) * picked, :], total)
            by_slope[b, :, at : at + width] = total
        whole = by_slope[b]
        high = whole.astype(jnp.bfloat16)
        low = (whole - high.astype(jnp.float32)).astype(jnp.bfloat16)
        folded = jnp.dot(high, fold_ref[...], preferred_element_type=jnp.float32)
        folded = folded + jnp.dot(low, fold_ref[...], preferred_element_type=jnp.float32)
        for core in range(CORES):
            series[core * PAIR + b] = folded[core * SLOTS : (core + 1) * SLOTS]
    lane = lax.broadcasted_iota(jnp.int32, (SLOTS, 128), 1) // 32
    at = 0
    for delay in range(MAXD + 1):
        first = first_slope(delay)
        size = SLOTS - first
        packed = jnp.zeros((size, 128), jnp.float32)
        for b in range(HELD):
            rows = series[b][first:, :]
            shift = (32 * b - delay) % 128
            rows = pltpu.roll(rows, shift, 1) if shift else rows
            packed = jnp.where(lane[:size] == b, rows, packed)
        stack[at : at + size, :] = packed
        at += size
    shifted = stack[...]
    high = shifted.astype(jnp.bfloat16)
    low = (shifted - high.astype(jnp.float32)).astype(jnp.bfloat16)
    result = jnp.dot(trial_ref[...], high, preferred_element_type=jnp.float32)
    result = result + jnp.dot(trial_ref[...], low, preferred_element_type=jnp.float32)
    turned = (result * scale_ref[0, 0]).T
    for q in range(POL):
        rolled = pltpu.roll(turned, 128 - 32 * q, 1) if q else turned
        for core in range(CORES):
            for b in range(PAIR):
                start = 32 * (core * PAIR + b)
                out_ref[core * POL + q, b] = rolled[start : start + TOUT]


def dedisperse(scale, normed, hot):
    return pl.pallas_call(
        dedisperse_kernel,
        in_specs=[SMEM, VMEM, VMEM, VMEM, VMEM],
        out_specs=VMEM,
        out_shape=jax.ShapeDtypeStruct((CORES * POL, PAIR, TOUT, 128), jnp.float32),
        scratch_shapes=[
            pltpu.VMEM((PAIR, CORES * SLOTS, UP * FR), jnp.float32),
            pltpu.VMEM((STACK, 128), jnp.float32),
        ],
        compiler_params=PARAMS,
        name="dedisperse",
    )(scale, normed, hot, jnp.asarray(fold_matrix()), jnp.asarray(trial_matrix()))


def slope_picker(slopes, mask, core):
    marked = jnp.where(mask != 0, slopes, -1).reshape(CHIPS, CORES, UP)
    marked = lax.dynamic_index_in_dim(marked, core, 1, keepdims=False).T.reshape(UP // 2, 2 * CHIPS)
    marked = jnp.repeat(marked, CORES, axis=1)[:, None, None, :]
    slope = jnp.arange(SLOTS, dtype=jnp.int32)[None, None, :, None]
    own = jnp.arange(CORES, dtype=jnp.int32)[None, :, None, None]
    column = jnp.arange(2 * FREQ, dtype=jnp.int32)[None, None, None, :]
    hot = (marked == slope) & (column % CORES == own)
    return hot.astype(jnp.bfloat16).reshape(UP // 2 * CORES * SLOTS, 2 * FREQ)


def on_device(voltages, gains, slopes, mask):
    me = lax.axis_index("pol")
    core = lax.axis_index("freq") % CORES
    tables = jnp.asarray(beam_tables())
    bank = jnp.asarray(bank_matrix())
    index = [(me + ahead) % POL for ahead in range(POL)]

    def send(power, ahead):
        return lax.ppermute(power, "pol", [(i, (i + ahead) % POL) for i in range(POL)])

    calibrated = calibrate(voltages[0, 0], gains[0, 0])
    parts, totals = [], 0.0
    for ahead in (2, 1, 3):
        power, total = quarter_powers([index[ahead]], calibrated, tables, bank)
        parts.append(send(power, ahead))
        totals = totals + total
    own, total = quarter_powers([index[0]], calibrated, tables, bank)
    normed = normalize(lax.psum(totals + total, "pol"), parts + [own])
    alike = [[CORES * chip + c for chip in range(CHIPS)] for c in range(CORES)]
    turned = lax.all_to_all(
        normed.reshape(CHIPS, CORES, PAIR * UP * FR), "freq", 0, 0, tiled=True, axis_index_groups=alike
    )
    scale = lax.rsqrt(jnp.sum(mask).astype(jnp.float32)).reshape(1, 1)
    out = dedisperse(scale, turned.reshape(FREQ, PAIR * UP * FR), slope_picker(slopes, mask, core))
    near = [
        [(CORES * chip + c) * POL + q for c in range(CORES) for q in range(POL)] for chip in range(CHIPS)
    ]
    out = lax.all_to_all(out, ("freq", "pol"), 0, 0, tiled=True, axis_index_groups=near)
    out = out[:POL] + out[POL:]
    return out.reshape(POL * PAIR, TOUT, 128)[:, :, : DM // POL]


def solution(mesh):
    placed = (P("freq", "pol", None, None, None), P("freq", "pol", None, None), P(), P())
    return jax.shard_map(
        on_device, mesh=mesh, in_specs=placed, out_specs=P("freq", None, "pol"), check_vma=False
    )
```

```python
import functools
import math

import jax
import jax.numpy as jnp
import ml_dtypes
import numpy as np
from jax import lax
from jax.experimental import pallas as pl
from jax.experimental.pallas import tpu as pltpu
from jax.sharding import PartitionSpec as P

FEEDS = 512
BEAMS = 1024
UP = 16
TAPS = 16
DM = 96
MAXD = 48
TOUT = 24
FR = 72
TS = 1392
POL = 4
FREQ = 128
PAIR = BEAMS // (POL * FREQ)
QUARTER = FREQ * PAIR
MG = 8
BLOCKS = FR // MG
ROWS = UP * MG
SPAN = (MG - 1 + TAPS) * UP
SLOTS = 56
TILES = FEEDS // 128
KINDS = 2 * TILES
CHUNKS = ((0, 368), (368, 512), (880, 512))
CORES = 2
CHIPS = FREQ // CORES
HELD = CORES * PAIR
EPSILON = 1e-06
BF16 = ml_dtypes.bfloat16
VMEM_LIMIT = 32 * 1024 * 1024
WHOLE_VMEM = 48 * 1024 * 1024


@functools.lru_cache(None)
def beam_tables():
    n = np.arange(FEEDS)[:, None]
    f = np.arange(FREQ)[None, :]
    b = np.arange(PAIR)[:, None]
    scale = np.float32(1.0 / math.sqrt(FEEDS))
    out = []
    for q in range(POL):
        k = (f * (POL * PAIR) + q * PAIR + b).reshape(1, -1)
        angle = ((n * k) % BEAMS).astype(np.float32) * np.float32(2.0 * math.pi / BEAMS)
        c = np.cos(angle) * scale
        s = np.sin(angle) * scale
        top = np.concatenate([c, -s], axis=1)
        low = np.concatenate([s, c], axis=1)
        out.append(np.concatenate([top, low], axis=0))
    return np.stack(out).astype(BF16)


@functools.lru_cache(None)
def bank_matrix():
    length = TAPS * UP
    pos = np.arange(length, dtype=np.float64) + 0.5
    hann = 0.5 - 0.5 * np.cos(2.0 * math.pi * pos / length)
    taps = (np.sinc((pos - 0.5 * length) / UP) * hann).astype(np.float32).astype(BF16)
    taps = taps.astype(np.float64)
    real = np.zeros((2, UP, MG, SPAN))
    imag = np.zeros((2, UP, MG, SPAN))
    lag = np.arange(length)
    for u in range(UP):
        angle = 2.0 * math.pi * ((u * lag) % UP) / UP
        c, s = taps * np.cos(angle), taps * np.sin(angle)
        for m in range(MG):
            at = slice(m * UP, m * UP + length)
            real[0, u, m, at], imag[0, u, m, at] = c, s
            real[1, u, m, at], imag[1, u, m, at] = -s, c
    both = np.concatenate([real.reshape(2 * ROWS, SPAN), imag.reshape(2 * ROWS, SPAN)], axis=1)
    return both.astype(np.float32).astype(BF16)


@functools.lru_cache(None)
def fold_matrix():
    g, u, m8 = np.meshgrid(np.arange(BLOCKS), np.arange(UP), np.arange(MG), indexing="ij")
    m = (g * MG + m8).reshape(-1)
    return (m[:, None] == np.arange(128)[None, :]).astype(np.float32).astype(BF16)


def first_slope(delay):
    return 8 * (delay // 8)


@functools.lru_cache(None)
def trial_matrix():
    parts = []
    share = DM // POL
    for delay in range(MAXD + 1):
        slope = np.arange(first_slope(delay), SLOTS)
        block = np.zeros((POL * 32, slope.size), np.float32)
        for d in range(DM):
            block[(d // share) * 32 + d % share] = ((d * slope) // (DM - 1) == delay) & (slope <= MAXD)
        parts.append(block)
    full = np.concatenate(parts, axis=1)
    return full.astype(BF16)


STACK = sum(SLOTS - first_slope(delay) for delay in range(MAXD + 1))


VMEM = pl.BlockSpec(memory_space=pltpu.VMEM)
SMEM = pl.BlockSpec(memory_space=pltpu.SMEM)
HBM = pl.BlockSpec(memory_space=pltpu.HBM)
PARAMS = pltpu.CompilerParams(vmem_limit_bytes=VMEM_LIMIT)
WHOLE = pltpu.CompilerParams(vmem_limit_bytes=WHOLE_VMEM)


def by_kind(block):
    samples = block.shape[0] // KINDS
    lifted = block.reshape(samples // 8, 8, KINDS, 128)
    parts = [lifted[:, t] for t in range(8)]
    row = lax.broadcasted_iota(jnp.int32, parts[0].shape, 1)
    for bit in (1, 2, 4):
        low = (row & bit) == 0
        for t in range(8):
            if t & bit == 0:
                a, b = parts[t], parts[t + bit]
                parts[t] = jnp.where(low, a, pltpu.roll(b, bit, 1))
                parts[t + bit] = jnp.where(low, pltpu.roll(a, 8 - bit, 1), b)
    return [part.reshape(samples, 128) for part in parts]


def calibrate_rows(v_ref, g_ref, cal_ref, start, size):
    kinds = by_kind(v_ref[start * KINDS : (start + size) * KINDS, :].astype(jnp.float32))
    rows = slice(start, start + size)
    for j in range(TILES):
        re, im = kinds[2 * j], kinds[2 * j + 1]
        lanes = slice(j * 128, (j + 1) * 128)
        gr = g_ref[0:1, lanes]
        gi = g_ref[1:2, lanes]
        cal_ref[rows, lanes] = (re * gr - im * gi).astype(jnp.bfloat16)
        lanes = slice(FEEDS + j * 128, FEEDS + (j + 1) * 128)
        cal_ref[rows, lanes] = (re * gi + im * gr).astype(jnp.bfloat16)


def form(cal_ref, tab_ref, formed, start, size):
    rows = slice(start, start + size)
    formed[rows, :] = jnp.dot(
        cal_ref[rows, :], tab_ref[...], preferred_element_type=jnp.float32
    ).astype(jnp.bfloat16)


def filter_power(bank_ref, formed, out_ref, tot_ref):
    total = jnp.zeros((ROWS, QUARTER), jnp.float32)
    for g in range(BLOCKS):
        rows = slice(g * ROWS, g * ROWS + SPAN)
        both = jnp.concatenate([formed[rows, :QUARTER], formed[rows, QUARTER:]], axis=0)
        fine = jnp.dot(bank_ref[...], both, preferred_element_type=jnp.float32)
        re, im = fine[:ROWS], fine[ROWS:]
        power = (re * re + im * im).astype(jnp.bfloat16)
        out_ref[g * ROWS : (g + 1) * ROWS, :] = power
        total = total + power.astype(jnp.float32)
    for u in range(UP):
        part = total[u * MG : (u + 1) * MG]
        tot_ref[u : u + 1, :] = jnp.broadcast_to(jnp.sum(part, keepdims=True), (1, 128))


def calibrate_kernel(v_hbm, g_hbm, cal_ref, v_ref, g_ref, sems):
    loads = []
    for i, (start, size) in enumerate(CHUNKS):
        rows = pl.ds(start * KINDS, size * KINDS)
        loads.append(pltpu.make_async_copy(v_hbm.at[rows, :], v_ref.at[rows, :], sems.at[i]))
    gains = pltpu.make_async_copy(g_hbm, g_ref, sems.at[len(CHUNKS)])
    for copy in [gains] + loads:
        copy.start()
    gains.wait()
    for copy, chunk in zip(loads, CHUNKS):
        copy.wait()
        calibrate_rows(v_ref, g_ref, cal_ref, *chunk)


def power_kernel(count, q_ref, cal_ref, tab_hbm, bank_ref, *refs):
    out_refs, tot_ref = refs[:count], refs[count]
    tab_ref, formed, tot_parts, tab_sems = refs[count + 1 :]
    tables = [
        pltpu.make_async_copy(tab_hbm.at[q_ref[n]], tab_ref.at[n], tab_sems.at[n]) for n in range(count)
    ]
    for copy in tables:
        copy.start()
    for n in range(count):
        tables[n].wait()
        for chunk in CHUNKS:
            form(cal_ref, tab_ref.at[n], formed.at[n], *chunk)
        filter_power(bank_ref, formed.at[n], out_refs[n], tot_parts.at[n])
    total = tot_parts[0]
    for n in range(1, count):
        total = total + tot_parts[n]
    tot_ref[...] = total


BRIEF = pl.CostEstimate(flops=100_000_000, bytes_accessed=10_000, transcendentals=0)
POWER = jax.ShapeDtypeStruct((UP * FR, QUARTER), jnp.bfloat16)
TOTAL = jax.ShapeDtypeStruct((UP, 128), jnp.float32)
def calibrate(voltages, gains):
    flat = voltages.reshape(TS, 2, TILES, 128).transpose(0, 2, 1, 3).reshape(TS * KINDS, 128)
    return pl.pallas_call(
        calibrate_kernel,
        in_specs=[HBM, HBM],
        out_specs=VMEM,
        out_shape=jax.ShapeDtypeStruct((TS, 2 * FEEDS), jnp.bfloat16),
        scratch_shapes=[
            pltpu.VMEM((TS * KINDS, 128), jnp.bfloat16),
            pltpu.VMEM((2, FEEDS), jnp.float32),
            pltpu.SemaphoreType.DMA((len(CHUNKS) + 1,)),
        ],
        compiler_params=pltpu.CompilerParams(vmem_limit_bytes=50 * 1024 * 1024),
        name="calibrate",
    )(flat, gains)


def quarter_powers(indices, calibrated, tables, bank):
    count = len(indices)
    return pl.pallas_call(
        functools.partial(power_kernel, count),
        in_specs=[SMEM, VMEM, HBM, VMEM],
        out_specs=[VMEM] * (count + 1),
        out_shape=[POWER] * count + [TOTAL],
        scratch_shapes=[
            pltpu.VMEM((count, 2 * FEEDS, 2 * QUARTER), jnp.bfloat16),
            pltpu.VMEM((count, TS, 2 * QUARTER), jnp.bfloat16),
            pltpu.VMEM((count, UP, 128), jnp.float32),
            pltpu.SemaphoreType.DMA((count,)),
        ],
        compiler_params=WHOLE,
        cost_estimate=BRIEF,
        name="quarter_powers",
    )(jnp.stack(indices), calibrated, tables, bank)


def normalize_kernel(tot_ref, a_ref, b_ref, c_ref, d_ref, out_ref, inverse):
    for u in range(UP):
        mean = tot_ref[u : u + 1, :] * (1.0 / (BEAMS * FR))
        inverse[u * MG : (u + 1) * MG, :] = jnp.broadcast_to(1.0 / (mean + EPSILON), (MG, 128))
    scale = inverse[...]
    for g in range(BLOCKS):
        rows = slice(g * ROWS, (g + 1) * ROWS)
        for b in range(PAIR):
            lanes = slice(b * FREQ, (b + 1) * FREQ)
            total = d_ref[rows, lanes].astype(jnp.float32)
            for ref in (a_ref, b_ref, c_ref):
                total = total + ref[rows, lanes].astype(jnp.float32)
            summed = total.astype(jnp.bfloat16).astype(jnp.float32)
            normed = summed * scale - 1.0
            at = b * UP * FR + g * ROWS
            out_ref[:, at : at + ROWS] = normed.T.astype(jnp.bfloat16)


def normalize(totals, parts):
    return pl.pallas_call(
        normalize_kernel,
        in_specs=[VMEM] * (1 + POL),
        out_specs=VMEM,
        out_shape=jax.ShapeDtypeStruct((FREQ, PAIR * UP * FR), jnp.bfloat16),
        scratch_shapes=[pltpu.VMEM((ROWS, 128), jnp.float32)],
        compiler_params=pltpu.CompilerParams(vmem_limit_bytes=60 * 1024 * 1024),
        name="normalize",
    )(totals, *parts)


def dedisperse_kernel(scale_ref, x_ref, hot_ref, fold_ref, trial_ref, out_ref, by_slope, stack):
    picked = CORES * SLOTS
    series = [None] * HELD
    for b in range(PAIR):
        for at in range(0, UP * FR, 256):
            width = min(256, UP * FR - at)
            start = b * UP * FR + at
            values = x_ref[:, start : start + width]
            fine = lax.broadcasted_iota(jnp.int32, values.shape, 1) // MG
            empty = jnp.zeros_like(values)
            even = jnp.where(fine % 2 == 0, values, empty)
            odd = jnp.where(fine % 2 == 0, empty, values)
            both = jnp.concatenate([even, odd], axis=0)
            product = jnp.dot(hot_ref[...], both, preferred_element_type=jnp.float32)
            couple = lax.broadcasted_iota(jnp.int32, (picked, width), 1) // (2 * MG) % (UP // 2)
            total = product[:picked, :]
            for n in range(1, UP // 2):
                total = jnp.where(couple == n, product[n * picked : (n + 1) * picked, :], total)
            by_slope[b, :, at : at + width] = total
        whole = by_slope[b]
        high = whole.astype(jnp.bfloat16)
        low = (whole - high.astype(jnp.float32)).astype(jnp.bfloat16)
        folded = jnp.dot(high, fold_ref[...], preferred_element_type=jnp.float32)
        folded = folded + jnp.dot(low, fold_ref[...], preferred_element_type=jnp.float32)
        for core in range(CORES):
            series[core * PAIR + b] = folded[core * SLOTS : (core + 1) * SLOTS]
    lane = lax.broadcasted_iota(jnp.int32, (SLOTS, 128), 1) // 32
    at = 0
    for delay in range(MAXD + 1):
        first = first_slope(delay)
        size = SLOTS - first
        packed = jnp.zeros((size, 128), jnp.float32)
        for b in range(HELD):
            rows = series[b][first:, :]
            shift = (32 * b - delay) % 128
            rows = pltpu.roll(rows, shift, 1) if shift else rows
            packed = jnp.where(lane[:size] == b, rows, packed)
        stack[at : at + size, :] = packed
        at += size
    shifted = stack[...]
    high = shifted.astype(jnp.bfloat16)
    low = (shifted - high.astype(jnp.float32)).astype(jnp.bfloat16)
    result = jnp.dot(trial_ref[...], high, preferred_element_type=jnp.float32)
    result = result + jnp.dot(trial_ref[...], low, preferred_element_type=jnp.float32)
    turned = (result * scale_ref[0, 0]).T
    for q in range(POL):
        rolled = pltpu.roll(turned, 128 - 32 * q, 1) if q else turned
        for core in range(CORES):
            for b in range(PAIR):
                start = 32 * (core * PAIR + b)
                out_ref[core * POL + q, b] = rolled[start : start + TOUT]


def dedisperse(scale, normed, hot):
    return pl.pallas_call(
        dedisperse_kernel,
        in_specs=[SMEM, VMEM, VMEM, VMEM, VMEM],
        out_specs=VMEM,
        out_shape=jax.ShapeDtypeStruct((CORES * POL, PAIR, TOUT, 128), jnp.float32),
        scratch_shapes=[
            pltpu.VMEM((PAIR, CORES * SLOTS, UP * FR), jnp.float32),
            pltpu.VMEM((STACK, 128), jnp.float32),
        ],
        compiler_params=PARAMS,
        name="dedisperse",
    )(scale, normed, hot, jnp.asarray(fold_matrix()), jnp.asarray(trial_matrix()))


def slope_picker(slopes, mask, core):
    marked = jnp.where(mask != 0, slopes, -1).reshape(CHIPS, CORES, UP)
    marked = lax.dynamic_index_in_dim(marked, core, 1, keepdims=False).T.reshape(UP // 2, 2 * CHIPS)
    marked = jnp.repeat(marked, CORES, axis=1)[:, None, None, :]
    slope = jnp.arange(SLOTS, dtype=jnp.int32)[None, None, :, None]
    own = jnp.arange(CORES, dtype=jnp.int32)[None, :, None, None]
    column = jnp.arange(2 * FREQ, dtype=jnp.int32)[None, None, None, :]
    hot = (marked == slope) & (column % CORES == own)
    return hot.astype(jnp.bfloat16).reshape(UP // 2 * CORES * SLOTS, 2 * FREQ)


def on_device(voltages, gains, slopes, mask):
    me = lax.axis_index("pol")
    core = lax.axis_index("freq") % CORES
    tables = jnp.asarray(beam_tables())
    bank = jnp.asarray(bank_matrix())
    index = [(me + ahead) % POL for ahead in range(POL)]

    def send(power, ahead):
        return lax.ppermute(power, "pol", [(i, (i + ahead) % POL) for i in range(POL)])

    calibrated = calibrate(voltages[0, 0], gains[0, 0])
    parts, totals = [], 0.0
    for ahead in (2, 1, 3):
        power, total = quarter_powers([index[ahead]], calibrated, tables, bank)
        parts.append(send(power, ahead))
        totals = totals + total
    own, total = quarter_powers([index[0]], calibrated, tables, bank)
    normed = normalize(lax.psum(totals + total, "pol"), parts + [own])
    alike = [[CORES * chip + c for chip in range(CHIPS)] for c in range(CORES)]
    turned = lax.all_to_all(
        normed.reshape(CHIPS, CORES, PAIR * UP * FR), "freq", 0, 0, tiled=True, axis_index_groups=alike
    )
    scale = lax.rsqrt(jnp.sum(mask).astype(jnp.float32)).reshape(1, 1)
    out = dedisperse(scale, turned.reshape(FREQ, PAIR * UP * FR), slope_picker(slopes, mask, core))
    near = [
        [(CORES * chip + c) * POL + q for c in range(CORES) for q in range(POL)] for chip in range(CHIPS)
    ]
    out = lax.all_to_all(out, ("freq", "pol"), 0, 0, tiled=True, axis_index_groups=near)
    out = out[:POL] + out[POL:]
    return out.reshape(POL * PAIR, TOUT, 128)[:, :, : DM // POL]


def solution(mesh):
    placed = (P("freq", "pol", None, None, None), P("freq", "pol", None, None), P(), P())
    return jax.shard_map(
        on_device, mesh=mesh, in_specs=placed, out_specs=P("freq", None, "pol"), check_vma=False
    )
```

```python
import functools
import math

import jax
import jax.numpy as jnp
import ml_dtypes
import numpy as np
from jax import lax
from jax.experimental import pallas as pl
from jax.experimental.pallas import tpu as pltpu
from jax.sharding import PartitionSpec as P

FEEDS = 512
BEAMS = 1024
UP = 16
TAPS = 16
DM = 96
MAXD = 48
TOUT = 24
FR = 72
TS = 1392
POL = 4
FREQ = 128
PAIR = BEAMS // (POL * FREQ)
QUARTER = FREQ * PAIR
MG = 8
BLOCKS = FR // MG
ROWS = UP * MG
SPAN = (MG - 1 + TAPS) * UP
SLOTS = 56
TILES = FEEDS // 128
KINDS = 2 * TILES
CHUNKS = ((0, 464), (464, 464), (928, 464))
CORES = 2
CHIPS = FREQ // CORES
HELD = CORES * PAIR
EPSILON = 1e-06
BF16 = ml_dtypes.bfloat16
VMEM_LIMIT = 32 * 1024 * 1024
WHOLE_VMEM = 48 * 1024 * 1024


@functools.lru_cache(None)
def beam_tables():
    n = np.arange(FEEDS)[:, None]
    f = np.arange(FREQ)[None, :]
    b = np.arange(PAIR)[:, None]
    scale = np.float32(1.0 / math.sqrt(FEEDS))
    out = []
    for q in range(POL):
        k = (f * (POL * PAIR) + q * PAIR + b).reshape(1, -1)
        angle = ((n * k) % BEAMS).astype(np.float32) * np.float32(2.0 * math.pi / BEAMS)
        c = np.cos(angle) * scale
        s = np.sin(angle) * scale
        top = np.concatenate([c, -s], axis=1)
        low = np.concatenate([s, c], axis=1)
        out.append(np.concatenate([top, low], axis=0))
    return np.stack(out).astype(BF16)


@functools.lru_cache(None)
def bank_matrix():
    length = TAPS * UP
    pos = np.arange(length, dtype=np.float64) + 0.5
    hann = 0.5 - 0.5 * np.cos(2.0 * math.pi * pos / length)
    taps = (np.sinc((pos - 0.5 * length) / UP) * hann).astype(np.float32).astype(BF16)
    taps = taps.astype(np.float64)
    real = np.zeros((2, UP, MG, SPAN))
    imag = np.zeros((2, UP, MG, SPAN))
    lag = np.arange(length)
    for u in range(UP):
        angle = 2.0 * math.pi * ((u * lag) % UP) / UP
        c, s = taps * np.cos(angle), taps * np.sin(angle)
        for m in range(MG):
            at = slice(m * UP, m * UP + length)
            real[0, u, m, at], imag[0, u, m, at] = c, s
            real[1, u, m, at], imag[1, u, m, at] = -s, c
    both = np.concatenate([real.reshape(2 * ROWS, SPAN), imag.reshape(2 * ROWS, SPAN)], axis=1)
    return both.astype(np.float32).astype(BF16)


@functools.lru_cache(None)
def fold_matrix():
    g, u, m8 = np.meshgrid(np.arange(BLOCKS), np.arange(UP), np.arange(MG), indexing="ij")
    m = (g * MG + m8).reshape(-1)
    return (m[:, None] == np.arange(128)[None, :]).astype(np.float32).astype(BF16)


def first_slope(delay):
    return 8 * (delay // 8)


@functools.lru_cache(None)
def trial_matrix():
    parts = []
    share = DM // POL
    for delay in range(MAXD + 1):
        slope = np.arange(first_slope(delay), SLOTS)
        block = np.zeros((POL * 32, slope.size), np.float32)
        for d in range(DM):
            block[(d // share) * 32 + d % share] = ((d * slope) // (DM - 1) == delay) & (slope <= MAXD)
        parts.append(block)
    full = np.concatenate(parts, axis=1)
    return full.astype(BF16)


STACK = sum(SLOTS - first_slope(delay) for delay in range(MAXD + 1))


VMEM = pl.BlockSpec(memory_space=pltpu.VMEM)
SMEM = pl.BlockSpec(memory_space=pltpu.SMEM)
HBM = pl.BlockSpec(memory_space=pltpu.HBM)
PARAMS = pltpu.CompilerParams(vmem_limit_bytes=VMEM_LIMIT)
WHOLE = pltpu.CompilerParams(vmem_limit_bytes=WHOLE_VMEM)


def by_kind(block):
    samples = block.shape[0] // KINDS
    lifted = block.reshape(samples // 8, 8, KINDS, 128)
    parts = [lifted[:, t] for t in range(8)]
    row = lax.broadcasted_iota(jnp.int32, parts[0].shape, 1)
    for bit in (1, 2, 4):
        low = (row & bit) == 0
        for t in range(8):
            if t & bit == 0:
                a, b = parts[t], parts[t + bit]
                parts[t] = jnp.where(low, a, pltpu.roll(b, bit, 1))
                parts[t + bit] = jnp.where(low, pltpu.roll(a, 8 - bit, 1), b)
    return [part.reshape(samples, 128) for part in parts]


def calibrate_rows(v_ref, g_ref, cal_ref, start, size):
    kinds = by_kind(v_ref[start * KINDS : (start + size) * KINDS, :].astype(jnp.float32))
    rows = slice(start, start + size)
    for j in range(TILES):
        re, im = kinds[2 * j], kinds[2 * j + 1]
        lanes = slice(j * 128, (j + 1) * 128)
        gr = g_ref[0:1, lanes]
        gi = g_ref[1:2, lanes]
        cal_ref[rows, lanes] = (re * gr - im * gi).astype(jnp.bfloat16)
        lanes = slice(FEEDS + j * 128, FEEDS + (j + 1) * 128)
        cal_ref[rows, lanes] = (re * gi + im * gr).astype(jnp.bfloat16)


def form(cal_ref, tab_ref, formed, start, size):
    rows = slice(start, start + size)
    formed[rows, :] = jnp.dot(
        cal_ref[rows, :], tab_ref[...], preferred_element_type=jnp.float32
    ).astype(jnp.bfloat16)


def filter_power(bank_ref, formed, out_ref, tot_ref):
    total = jnp.zeros((ROWS, QUARTER), jnp.float32)
    for g in range(BLOCKS):
        rows = slice(g * ROWS, g * ROWS + SPAN)
        both = jnp.concatenate([formed[rows, :QUARTER], formed[rows, QUARTER:]], axis=0)
        fine = jnp.dot(bank_ref[...], both, preferred_element_type=jnp.float32)
        re, im = fine[:ROWS], fine[ROWS:]
        power = (re * re + im * im).astype(jnp.bfloat16)
        out_ref[g * ROWS : (g + 1) * ROWS, :] = power
        total = total + power.astype(jnp.float32)
    for u in range(UP):
        part = total[u * MG : (u + 1) * MG]
        tot_ref[u : u + 1, :] = jnp.broadcast_to(jnp.sum(part, keepdims=True), (1, 128))


def calibrate_kernel(q_ref, v_ref, g_ref, tab_hbm, cal_ref, tab_ref, tab_sems):
    tables = [
        pltpu.make_async_copy(tab_hbm.at[q_ref[n]], tab_ref.at[n], tab_sems.at[n]) for n in range(POL)
    ]
    for copy in tables:
        copy.start()
    for chunk in CHUNKS:
        calibrate_rows(v_ref, g_ref, cal_ref, *chunk)
    for copy in tables:
        copy.wait()


def power_kernel(n, cal_ref, tab_ref, bank_ref, out_ref, tot_ref, formed):
    for chunk in CHUNKS:
        form(cal_ref, tab_ref.at[n], formed, *chunk)
    filter_power(bank_ref, formed, out_ref, tot_ref)


BRIEF = pl.CostEstimate(flops=100_000_000, bytes_accessed=10_000, transcendentals=0)
POWER = jax.ShapeDtypeStruct((UP * FR, QUARTER), jnp.bfloat16)
TOTAL = jax.ShapeDtypeStruct((UP, 128), jnp.float32)
def calibrate(order, voltages, gains, tables):
    flat = voltages.reshape(TS, 2, TILES, 128).transpose(0, 2, 1, 3).reshape(TS * KINDS, 128)
    return pl.pallas_call(
        calibrate_kernel,
        in_specs=[SMEM, VMEM, VMEM, HBM],
        out_specs=[VMEM, VMEM],
        out_shape=[
            jax.ShapeDtypeStruct((TS, 2 * FEEDS), jnp.bfloat16),
            jax.ShapeDtypeStruct((POL, 2 * FEEDS, 2 * QUARTER), jnp.bfloat16),
        ],
        scratch_shapes=[pltpu.SemaphoreType.DMA((POL,))],
        compiler_params=pltpu.CompilerParams(vmem_limit_bytes=44 * 1024 * 1024),
        name="calibrate",
    )(order, flat, gains, tables)


def quarter_power(n, calibrated, tables, bank):
    return pl.pallas_call(
        functools.partial(power_kernel, n),
        in_specs=[VMEM, VMEM, VMEM],
        out_specs=[VMEM, VMEM],
        out_shape=[POWER, TOTAL],
        scratch_shapes=[pltpu.VMEM((TS, 2 * QUARTER), jnp.bfloat16)],
        compiler_params=pltpu.CompilerParams(vmem_limit_bytes=32 * 1024 * 1024),
        cost_estimate=BRIEF,
        name="quarter_power",
    )(calibrated, tables, bank)


def normalize_kernel(tot_ref, a_ref, b_ref, c_ref, d_ref, out_ref, inverse):
    for u in range(UP):
        mean = tot_ref[u : u + 1, :] * (1.0 / (BEAMS * FR))
        inverse[u * MG : (u + 1) * MG, :] = jnp.broadcast_to(1.0 / (mean + EPSILON), (MG, 128))
    scale = inverse[...]
    for g in range(BLOCKS):
        rows = slice(g * ROWS, (g + 1) * ROWS)
        for b in range(PAIR):
            lanes = slice(b * FREQ, (b + 1) * FREQ)
            total = d_ref[rows, lanes].astype(jnp.float32)
            for ref in (a_ref, b_ref, c_ref):
                total = total + ref[rows, lanes].astype(jnp.float32)
            summed = total.astype(jnp.bfloat16).astype(jnp.float32)
            normed = summed * scale - 1.0
            at = b * UP * FR + g * ROWS
            out_ref[:, at : at + ROWS] = normed.T.astype(jnp.bfloat16)


def normalize(totals, parts):
    return pl.pallas_call(
        normalize_kernel,
        in_specs=[VMEM] * (1 + POL),
        out_specs=VMEM,
        out_shape=jax.ShapeDtypeStruct((FREQ, PAIR * UP * FR), jnp.bfloat16),
        scratch_shapes=[pltpu.VMEM((ROWS, 128), jnp.float32)],
        compiler_params=PARAMS,
        name="normalize",
    )(totals, *parts)


def dedisperse_kernel(scale_ref, x_ref, hot_ref, fold_ref, trial_ref, out_ref, by_slope, stack):
    picked = CORES * SLOTS
    series = [None] * HELD
    for b in range(PAIR):
        for at in range(0, UP * FR, 256):
            width = min(256, UP * FR - at)
            start = b * UP * FR + at
            values = x_ref[:, start : start + width]
            fine = lax.broadcasted_iota(jnp.int32, values.shape, 1) // MG
            empty = jnp.zeros_like(values)
            even = jnp.where(fine % 2 == 0, values, empty)
            odd = jnp.where(fine % 2 == 0, empty, values)
            both = jnp.concatenate([even, odd], axis=0)
            product = jnp.dot(hot_ref[...], both, preferred_element_type=jnp.float32)
            couple = lax.broadcasted_iota(jnp.int32, (picked, width), 1) // (2 * MG) % (UP // 2)
            total = product[:picked, :]
            for n in range(1, UP // 2):
                total = jnp.where(couple == n, product[n * picked : (n + 1) * picked, :], total)
            by_slope[b, :, at : at + width] = total
        whole = by_slope[b]
        high = whole.astype(jnp.bfloat16)
        low = (whole - high.astype(jnp.float32)).astype(jnp.bfloat16)
        folded = jnp.dot(high, fold_ref[...], preferred_element_type=jnp.float32)
        folded = folded + jnp.dot(low, fold_ref[...], preferred_element_type=jnp.float32)
        for core in range(CORES):
            series[core * PAIR + b] = folded[core * SLOTS : (core + 1) * SLOTS]
    lane = lax.broadcasted_iota(jnp.int32, (SLOTS, 128), 1) // 32
    at = 0
    for delay in range(MAXD + 1):
        first = first_slope(delay)
        size = SLOTS - first
        packed = jnp.zeros((size, 128), jnp.float32)
        for b in range(HELD):
            rows = series[b][first:, :]
            shift = (32 * b - delay) % 128
            rows = pltpu.roll(rows, shift, 1) if shift else rows
            packed = jnp.where(lane[:size] == b, rows, packed)
        stack[at : at + size, :] = packed
        at += size
    shifted = stack[...]
    high = shifted.astype(jnp.bfloat16)
    low = (shifted - high.astype(jnp.float32)).astype(jnp.bfloat16)
    result = jnp.dot(trial_ref[...], high, preferred_element_type=jnp.float32)
    result = result + jnp.dot(trial_ref[...], low, preferred_element_type=jnp.float32)
    turned = (result * scale_ref[0, 0]).T
    for q in range(POL):
        rolled = pltpu.roll(turned, 128 - 32 * q, 1) if q else turned
        for core in range(CORES):
            for b in range(PAIR):
                start = 32 * (core * PAIR + b)
                out_ref[core * POL + q, b] = rolled[start : start + TOUT]


def dedisperse(scale, normed, hot):
    return pl.pallas_call(
        dedisperse_kernel,
        in_specs=[SMEM, VMEM, VMEM, VMEM, VMEM],
        out_specs=VMEM,
        out_shape=jax.ShapeDtypeStruct((CORES * POL, PAIR, TOUT, 128), jnp.float32),
        scratch_shapes=[
            pltpu.VMEM((PAIR, CORES * SLOTS, UP * FR), jnp.float32),
            pltpu.VMEM((STACK, 128), jnp.float32),
        ],
        compiler_params=PARAMS,
        name="dedisperse",
    )(scale, normed, hot, jnp.asarray(fold_matrix()), jnp.asarray(trial_matrix()))


def slope_picker(slopes, mask, core):
    marked = jnp.where(mask != 0, slopes, -1).reshape(CHIPS, CORES, UP)
    marked = lax.dynamic_index_in_dim(marked, core, 1, keepdims=False).T.reshape(UP // 2, 2 * CHIPS)
    marked = jnp.repeat(marked, CORES, axis=1)[:, None, None, :]
    slope = jnp.arange(SLOTS, dtype=jnp.int32)[None, None, :, None]
    own = jnp.arange(CORES, dtype=jnp.int32)[None, :, None, None]
    column = jnp.arange(2 * FREQ, dtype=jnp.int32)[None, None, None, :]
    hot = (marked == slope) & (column % CORES == own)
    return hot.astype(jnp.bfloat16).reshape(UP // 2 * CORES * SLOTS, 2 * FREQ)


def on_device(voltages, gains, slopes, mask):
    me = lax.axis_index("pol")
    core = lax.axis_index("freq") % CORES
    tables = jnp.asarray(beam_tables())
    bank = jnp.asarray(bank_matrix())
    order = (2, 1, 3, 0)

    def send(power, ahead):
        return lax.ppermute(power, "pol", [(i, (i + ahead) % POL) for i in range(POL)])

    whose = (me + jnp.array(order, jnp.int32)) % POL
    calibrated, tables = calibrate(whose, voltages[0, 0], gains[0, 0], tables)
    parts, totals = [], 0.0
    for n, ahead in enumerate(order):
        power, total = quarter_power(n, calibrated, tables, bank)
        parts.append(send(power, ahead) if ahead else power)
        totals = totals + total
    normed = normalize(lax.psum(totals, "pol"), parts)
    alike = [[CORES * chip + c for chip in range(CHIPS)] for c in range(CORES)]
    turned = lax.all_to_all(
        normed.reshape(CHIPS, CORES, PAIR * UP * FR), "freq", 0, 0, tiled=True, axis_index_groups=alike
    )
    scale = lax.rsqrt(jnp.sum(mask).astype(jnp.float32)).reshape(1, 1)
    out = dedisperse(scale, turned.reshape(FREQ, PAIR * UP * FR), slope_picker(slopes, mask, core))
    near = [
        [(CORES * chip + c) * POL + q for c in range(CORES) for q in range(POL)] for chip in range(CHIPS)
    ]
    out = lax.all_to_all(out, ("freq", "pol"), 0, 0, tiled=True, axis_index_groups=near)
    out = out[:POL] + out[POL:]
    return out.reshape(POL * PAIR, TOUT, 128)[:, :, : DM // POL]


def solution(mesh):
    placed = (P("freq", "pol", None, None, None), P("freq", "pol", None, None), P(), P())
    return jax.shard_map(
        on_device, mesh=mesh, in_specs=placed, out_specs=P("freq", None, "pol"), check_vma=False
    )
```

```python
import functools
import math

import jax
import jax.numpy as jnp
import ml_dtypes
import numpy as np
from jax import lax
from jax.experimental import pallas as pl
from jax.experimental.pallas import tpu as pltpu
from jax.sharding import PartitionSpec as P

FEEDS = 512
BEAMS = 1024
UP = 16
TAPS = 16
DM = 96
MAXD = 48
TOUT = 24
FR = 72
TS = 1392
POL = 4
FREQ = 128
PAIR = BEAMS // (POL * FREQ)
QUARTER = FREQ * PAIR
MG = 8
BLOCKS = FR // MG
ROWS = UP * MG
SPAN = (MG - 1 + TAPS) * UP
SLOTS = 56
TILES = FEEDS // 128
KINDS = 2 * TILES
CHUNKS = ((0, 464), (464, 464), (928, 464))
CORES = 2
CHIPS = FREQ // CORES
HELD = CORES * PAIR
EPSILON = 1e-06
BF16 = ml_dtypes.bfloat16
VMEM_LIMIT = 32 * 1024 * 1024
WHOLE_VMEM = 48 * 1024 * 1024


@functools.lru_cache(None)
def beam_tables():
    n = np.arange(FEEDS)[:, None]
    f = np.arange(FREQ)[None, :]
    b = np.arange(PAIR)[:, None]
    scale = np.float32(1.0 / math.sqrt(FEEDS))
    out = []
    for q in range(POL):
        k = (f * (POL * PAIR) + q * PAIR + b).reshape(1, -1)
        angle = ((n * k) % BEAMS).astype(np.float32) * np.float32(2.0 * math.pi / BEAMS)
        c = np.cos(angle) * scale
        s = np.sin(angle) * scale
        top = np.concatenate([c, -s], axis=1)
        low = np.concatenate([s, c], axis=1)
        out.append(np.concatenate([top, low], axis=0))
    return np.stack(out).astype(BF16)


@functools.lru_cache(None)
def bank_matrix():
    length = TAPS * UP
    pos = np.arange(length, dtype=np.float64) + 0.5
    hann = 0.5 - 0.5 * np.cos(2.0 * math.pi * pos / length)
    taps = (np.sinc((pos - 0.5 * length) / UP) * hann).astype(np.float32).astype(BF16)
    taps = taps.astype(np.float64)
    real = np.zeros((2, UP, MG, SPAN))
    imag = np.zeros((2, UP, MG, SPAN))
    lag = np.arange(length)
    for u in range(UP):
        angle = 2.0 * math.pi * ((u * lag) % UP) / UP
        c, s = taps * np.cos(angle), taps * np.sin(angle)
        for m in range(MG):
            at = slice(m * UP, m * UP + length)
            real[0, u, m, at], imag[0, u, m, at] = c, s
            real[1, u, m, at], imag[1, u, m, at] = -s, c
    both = np.concatenate([real.reshape(2 * ROWS, SPAN), imag.reshape(2 * ROWS, SPAN)], axis=1)
    return both.astype(np.float32).astype(BF16)


@functools.lru_cache(None)
def fold_matrix():
    g, u, m8 = np.meshgrid(np.arange(BLOCKS), np.arange(UP), np.arange(MG), indexing="ij")
    m = (g * MG + m8).reshape(-1)
    return (m[:, None] == np.arange(128)[None, :]).astype(np.float32).astype(BF16)


def first_slope(delay):
    return 8 * (delay // 8)


@functools.lru_cache(None)
def trial_matrix():
    parts = []
    share = DM // POL
    for delay in range(MAXD + 1):
        slope = np.arange(first_slope(delay), SLOTS)
        block = np.zeros((POL * 32, slope.size), np.float32)
        for d in range(DM):
            block[(d // share) * 32 + d % share] = ((d * slope) // (DM - 1) == delay) & (slope <= MAXD)
        parts.append(block)
    full = np.concatenate(parts, axis=1)
    return full.astype(BF16)


STACK = sum(SLOTS - first_slope(delay) for delay in range(MAXD + 1))


VMEM = pl.BlockSpec(memory_space=pltpu.VMEM)
SMEM = pl.BlockSpec(memory_space=pltpu.SMEM)
HBM = pl.BlockSpec(memory_space=pltpu.HBM)
PARAMS = pltpu.CompilerParams(vmem_limit_bytes=VMEM_LIMIT)
WHOLE = pltpu.CompilerParams(vmem_limit_bytes=WHOLE_VMEM)


def by_kind(block):
    samples = block.shape[0] // KINDS
    lifted = block.reshape(samples // 8, 8, KINDS, 128)
    parts = [lifted[:, t] for t in range(8)]
    row = lax.broadcasted_iota(jnp.int32, parts[0].shape, 1)
    for bit in (1, 2, 4):
        low = (row & bit) == 0
        for t in range(8):
            if t & bit == 0:
                a, b = parts[t], parts[t + bit]
                parts[t] = jnp.where(low, a, pltpu.roll(b, bit, 1))
                parts[t + bit] = jnp.where(low, pltpu.roll(a, 8 - bit, 1), b)
    return [part.reshape(samples, 128) for part in parts]


def calibrate_rows(v_ref, g_ref, cal_ref, start, size):
    kinds = by_kind(v_ref[start * KINDS : (start + size) * KINDS, :].astype(jnp.float32))
    rows = slice(start, start + size)
    for j in range(TILES):
        re, im = kinds[2 * j], kinds[2 * j + 1]
        lanes = slice(j * 128, (j + 1) * 128)
        gr = g_ref[0:1, lanes]
        gi = g_ref[1:2, lanes]
        cal_ref[rows, lanes] = (re * gr - im * gi).astype(jnp.bfloat16)
        lanes = slice(FEEDS + j * 128, FEEDS + (j + 1) * 128)
        cal_ref[rows, lanes] = (re * gi + im * gr).astype(jnp.bfloat16)


def form(cal_ref, tab_ref, formed, start, size):
    rows = slice(start, start + size)
    formed[rows, :] = jnp.dot(
        cal_ref[rows, :], tab_ref[...], preferred_element_type=jnp.float32
    ).astype(jnp.bfloat16)


def filter_power(bank_ref, formed, out_ref, tot_ref):
    total = jnp.zeros((ROWS, QUARTER), jnp.float32)
    for g in range(BLOCKS):
        rows = slice(g * ROWS, g * ROWS + SPAN)
        both = jnp.concatenate([formed[rows, :QUARTER], formed[rows, QUARTER:]], axis=0)
        fine = jnp.dot(bank_ref[...], both, preferred_element_type=jnp.float32)
        re, im = fine[:ROWS], fine[ROWS:]
        power = (re * re + im * im).astype(jnp.bfloat16)
        out_ref[g * ROWS : (g + 1) * ROWS, :] = power
        total = total + power.astype(jnp.float32)
    for u in range(UP):
        part = total[u * MG : (u + 1) * MG]
        tot_ref[u : u + 1, :] = jnp.broadcast_to(jnp.sum(part, keepdims=True), (1, 128))


ORDER = (2, 1, 3, 0)


def calibrate_kernel(q_ref, v_ref, g_ref, tab_hbm, cal_ref, tab_ref, tab_sems):
    tables = [
        pltpu.make_async_copy(tab_hbm.at[(q_ref[0] + ahead) % POL], tab_ref.at[n], tab_sems.at[n])
        for n, ahead in enumerate(ORDER)
    ]
    for copy in tables:
        copy.start()
    for chunk in CHUNKS:
        calibrate_rows(v_ref, g_ref, cal_ref, *chunk)
    for copy in tables:
        copy.wait()


def power_kernel(n, cal_ref, tab_ref, bank_ref, out_ref, tot_ref, formed):
    for chunk in CHUNKS:
        form(cal_ref, tab_ref.at[n], formed, *chunk)
    filter_power(bank_ref, formed, out_ref, tot_ref)


BRIEF = pl.CostEstimate(flops=100_000_000, bytes_accessed=10_000, transcendentals=0)
POWER = jax.ShapeDtypeStruct((UP * FR, QUARTER), jnp.bfloat16)
TOTAL = jax.ShapeDtypeStruct((UP, 128), jnp.float32)
def calibrate(order, voltages, gains, tables):
    flat = voltages.reshape(TS, 2, TILES, 128).transpose(0, 2, 1, 3).reshape(TS * KINDS, 128)
    return pl.pallas_call(
        calibrate_kernel,
        in_specs=[SMEM, VMEM, VMEM, HBM],
        out_specs=[VMEM, VMEM],
        out_shape=[
            jax.ShapeDtypeStruct((TS, 2 * FEEDS), jnp.bfloat16),
            jax.ShapeDtypeStruct((POL, 2 * FEEDS, 2 * QUARTER), jnp.bfloat16),
        ],
        scratch_shapes=[pltpu.SemaphoreType.DMA((POL,))],
        compiler_params=pltpu.CompilerParams(vmem_limit_bytes=44 * 1024 * 1024),
        name="calibrate",
    )(order, flat, gains, tables)


def quarter_power(n, calibrated, tables, bank):
    return pl.pallas_call(
        functools.partial(power_kernel, n),
        in_specs=[VMEM, VMEM, VMEM],
        out_specs=[VMEM, VMEM],
        out_shape=[POWER, TOTAL],
        scratch_shapes=[pltpu.VMEM((TS, 2 * QUARTER), jnp.bfloat16)],
        compiler_params=pltpu.CompilerParams(vmem_limit_bytes=32 * 1024 * 1024),
        cost_estimate=BRIEF,
        name="quarter_power",
    )(calibrated, tables, bank)


def normalize_kernel(tot_ref, a_ref, b_ref, c_ref, d_ref, out_ref, inverse):
    means = (tot_ref[0] + tot_ref[1] + tot_ref[2] + tot_ref[3]) * (1.0 / (BEAMS * FR))
    for u in range(UP):
        mean = means[u : u + 1, :]
        inverse[u * MG : (u + 1) * MG, :] = jnp.broadcast_to(1.0 / (mean + EPSILON), (MG, 128))
    scale = inverse[...]
    for g in range(BLOCKS):
        rows = slice(g * ROWS, (g + 1) * ROWS)
        for b in range(PAIR):
            lanes = slice(b * FREQ, (b + 1) * FREQ)
            total = d_ref[rows, lanes].astype(jnp.float32)
            for ref in (a_ref, b_ref, c_ref):
                total = total + ref[rows, lanes].astype(jnp.float32)
            summed = total.astype(jnp.bfloat16).astype(jnp.float32)
            normed = summed * scale - 1.0
            at = b * UP * FR + g * ROWS
            out_ref[:, at : at + ROWS] = normed.T.astype(jnp.bfloat16)


def normalize(totals, parts):
    return pl.pallas_call(
        normalize_kernel,
        in_specs=[VMEM] * (1 + POL),
        out_specs=VMEM,
        out_shape=jax.ShapeDtypeStruct((FREQ, PAIR * UP * FR), jnp.bfloat16),
        scratch_shapes=[pltpu.VMEM((ROWS, 128), jnp.float32)],
        compiler_params=PARAMS,
        name="normalize",
    )(totals, *parts)


def dedisperse_kernel(scale_ref, x_ref, hot_ref, fold_ref, trial_ref, out_ref, by_slope, stack):
    picked = CORES * SLOTS
    series = [None] * HELD
    for b in range(PAIR):
        for at in range(0, UP * FR, 256):
            width = min(256, UP * FR - at)
            start = b * UP * FR + at
            values = x_ref[:, start : start + width]
            fine = lax.broadcasted_iota(jnp.int32, values.shape, 1) // MG
            empty = jnp.zeros_like(values)
            even = jnp.where(fine % 2 == 0, values, empty)
            odd = jnp.where(fine % 2 == 0, empty, values)
            both = jnp.concatenate([even, odd], axis=0)
            product = jnp.dot(hot_ref[...], both, preferred_element_type=jnp.float32)
            couple = lax.broadcasted_iota(jnp.int32, (picked, width), 1) // (2 * MG) % (UP // 2)
            total = product[:picked, :]
            for n in range(1, UP // 2):
                total = jnp.where(couple == n, product[n * picked : (n + 1) * picked, :], total)
            by_slope[b, :, at : at + width] = total
        whole = by_slope[b]
        high = whole.astype(jnp.bfloat16)
        low = (whole - high.astype(jnp.float32)).astype(jnp.bfloat16)
        folded = jnp.dot(high, fold_ref[...], preferred_element_type=jnp.float32)
        folded = folded + jnp.dot(low, fold_ref[...], preferred_element_type=jnp.float32)
        for core in range(CORES):
            series[core * PAIR + b] = folded[core * SLOTS : (core + 1) * SLOTS]
    lane = lax.broadcasted_iota(jnp.int32, (SLOTS, 128), 1) // 32
    at = 0
    for delay in range(MAXD + 1):
        first = first_slope(delay)
        size = SLOTS - first
        packed = jnp.zeros((size, 128), jnp.float32)
        for b in range(HELD):
            rows = series[b][first:, :]
            shift = (32 * b - delay) % 128
            rows = pltpu.roll(rows, shift, 1) if shift else rows
            packed = jnp.where(lane[:size] == b, rows, packed)
        stack[at : at + size, :] = packed
        at += size
    shifted = stack[...]
    high = shifted.astype(jnp.bfloat16)
    low = (shifted - high.astype(jnp.float32)).astype(jnp.bfloat16)
    result = jnp.dot(trial_ref[...], high, preferred_element_type=jnp.float32)
    result = result + jnp.dot(trial_ref[...], low, preferred_element_type=jnp.float32)
    turned = (result * scale_ref[0, 0]).T
    for q in range(POL):
        rolled = pltpu.roll(turned, 128 - 32 * q, 1) if q else turned
        for core in range(CORES):
            for b in range(PAIR):
                start = 32 * (core * PAIR + b)
                out_ref[core * POL + q, b] = rolled[start : start + TOUT]


def dedisperse(scale, normed, hot):
    return pl.pallas_call(
        dedisperse_kernel,
        in_specs=[SMEM, VMEM, VMEM, VMEM, VMEM],
        out_specs=VMEM,
        out_shape=jax.ShapeDtypeStruct((CORES * POL, PAIR, TOUT, 128), jnp.float32),
        scratch_shapes=[
            pltpu.VMEM((PAIR, CORES * SLOTS, UP * FR), jnp.float32),
            pltpu.VMEM((STACK, 128), jnp.float32),
        ],
        compiler_params=PARAMS,
        name="dedisperse",
    )(scale, normed, hot, jnp.asarray(fold_matrix()), jnp.asarray(trial_matrix()))


def slope_picker(slopes, mask, core):
    marked = jnp.where(mask != 0, slopes, -1).reshape(CHIPS, CORES, UP)
    marked = lax.dynamic_index_in_dim(marked, core, 1, keepdims=False).T.reshape(UP // 2, 2 * CHIPS)
    marked = jnp.repeat(marked, CORES, axis=1)[:, None, None, :]
    slope = jnp.arange(SLOTS, dtype=jnp.int32)[None, None, :, None]
    own = jnp.arange(CORES, dtype=jnp.int32)[None, :, None, None]
    column = jnp.arange(2 * FREQ, dtype=jnp.int32)[None, None, None, :]
    hot = (marked == slope) & (column % CORES == own)
    return hot.astype(jnp.bfloat16).reshape(UP // 2 * CORES * SLOTS, 2 * FREQ)


def on_device(voltages, gains, slopes, mask):
    me = lax.axis_index("pol")
    core = lax.axis_index("freq") % CORES
    tables = jnp.asarray(beam_tables())
    bank = jnp.asarray(bank_matrix())
    def send(power, ahead):
        return lax.ppermute(power, "pol", [(i, (i + ahead) % POL) for i in range(POL)])

    calibrated, tables = calibrate(me.reshape(1), voltages[0, 0], gains[0, 0], tables)
    parts, totals = [], 0.0
    for n, ahead in enumerate(ORDER):
        power, total = quarter_power(n, calibrated, tables, bank)
        parts.append(send(power, ahead) if ahead else power)
        totals = totals + total
    normed = normalize(lax.all_to_all(jnp.broadcast_to(totals, (POL, UP, 128)), "pol", 0, 0, tiled=True), parts)
    alike = [[CORES * chip + c for chip in range(CHIPS)] for c in range(CORES)]
    turned = lax.all_to_all(
        normed.reshape(CHIPS, CORES, PAIR * UP * FR), "freq", 0, 0, tiled=True, axis_index_groups=alike
    )
    scale = lax.rsqrt(jnp.sum(mask).astype(jnp.float32)).reshape(1, 1)
    out = dedisperse(scale, turned.reshape(FREQ, PAIR * UP * FR), slope_picker(slopes, mask, core))
    near = [
        [(CORES * chip + c) * POL + q for c in range(CORES) for q in range(POL)] for chip in range(CHIPS)
    ]
    out = lax.all_to_all(out, ("freq", "pol"), 0, 0, tiled=True, axis_index_groups=near)
    out = out[:POL] + out[POL:]
    return out.reshape(POL * PAIR, TOUT, 128)[:, :, : DM // POL]


def solution(mesh):
    placed = (P("freq", "pol", None, None, None), P("freq", "pol", None, None), P(), P())
    return jax.shard_map(
        on_device, mesh=mesh, in_specs=placed, out_specs=P("freq", None, "pol"), check_vma=False
    )
```
